32 devices in a mesh: elec: 4 (over z), cell: 8 (over y, x, core).
Axes of the slice: x: 2, y: 2, z: 4, core: 2. Of those that a mesh axis runs over, the one named last changes fastest.
Arguments:
- grads: bfloat16 [3, 1024, 1024], P(None, 'elec', 'cell'), may hold values from -6 to 6
- quads: int32 [16384, 4], P('elec'), may hold values from 0 to 1023, all different within a row
- volume: float32 [1024], P('cell'), may hold values from 0.5 to 2
- weight: float32 [16384], P('elec'), may hold values from 0.5 to 2
Outputs:
- hessian: float32 [1024, 1024], P('elec', 'cell')
The draws below stay inside these ranges and needn't reach their ends.
Inputs may be any that keep to these rules, and one draw needn't show every extreme that they name: `quads`: each row names four different electrodes; every electrode appears in some row.
All inputs are finite; a program needn't handle non-finite values.
Results may differ from the reference program's by a relative error of at most 0.00096.
Values may be sent and summed in bfloat16 or wider, within the bound.
No kernel may reach another device: no remote copies, remote signals or barrier semaphores. Data moves between devices by JAX's collectives and lax.ppermute only.
A program may use at most 64 MiB of HBM per device.

```python
import math
import jax
import jax.numpy as jnp
from jax import lax

ELECTRODE_COUNT = 1024
SLAB_CELLS = 1024
MEASURE_TOTAL = 16384


def steps_of(own_key, dims, shards, low, largest):
    factor_of, own = 1.0, jax.random.fold_in(own_key, 6)
    for axis_at, blocks in shards:
        steps = jnp.exp(jax.random.uniform(jax.random.fold_in(own, axis_at), (blocks,), jnp.float32, low / len(shards), largest / len(shards)))
        factor_of = factor_of * jnp.repeat(steps, dims[axis_at] // blocks).reshape([-1 if axis == axis_at else 1 for axis in range(len(dims))])
    return factor_of


def distinct(own_key, rows, amount, top, lift):
    order = jax.random.permutation(jax.random.fold_in(own_key, 1), amount)
    pull = order
    for power in range(3):
        pull = pull * pull // amount
    pull = pull * lift // amount
    lots = jax.random.randint(jax.random.fold_in(own_key, 2), (rows, amount), 0, 4096) + pull
    sure = jax.random.permutation(jax.random.fold_in(own_key, 3), rows)[jnp.arange(amount) % rows]
    lots = jnp.where(jnp.arange(rows)[:, None] == sure[None, :], 1 << 14, lots)
    merit = lots * amount + jnp.arange(amount)
    return lax.top_k(merit.astype(jnp.int32), top)[1].astype(jnp.int32)


def gaussian(stream_key, extent, deviation, most, split=(), dtype=jnp.bfloat16):
    array = deviation * jax.random.normal(stream_key, extent, jnp.float32)
    if split:
        array = array * steps_of(stream_key, extent, split, -0.22, 0.18)
    return jnp.clip(array, -most, most).astype(dtype)


def setup_inputs(seed: int = 0) -> dict:
    streams_of = jax.random.split(jax.random.key(seed), 5)
    grads = gaussian(streams_of[0], (3, ELECTRODE_COUNT, SLAB_CELLS), 1.0, 6.0, ((1, 4), (2, 8)))
    quads = distinct(streams_of[1], MEASURE_TOTAL, ELECTRODE_COUNT, 4, 0)
    volume = jnp.clip(jnp.exp(math.log(2.0) - 1.3862944 * jax.random.uniform(streams_of[2], (SLAB_CELLS,), jnp.float32) ** steps_of(streams_of[2], (SLAB_CELLS,), ((0, 8),), -0.2, 0.2)), 0.5, 2.0)
    weight = jnp.clip(jnp.exp(math.log(2.0) - 1.3862944 * jax.random.uniform(streams_of[3], (MEASURE_TOTAL,), jnp.float32) ** steps_of(streams_of[3], (MEASURE_TOTAL,), ((0, 4),), -0.2, 0.2)), 0.5, 2.0)
    return dict(grads=grads, quads=quads, volume=volume, weight=weight)


def reference(grads, quads, volume, weight):
    field = grads.astype(jnp.float32)
    rows_of_block = math.gcd(MEASURE_TOTAL, 1024)

    def single_block(index):
        begin = (index * rows_of_block).astype(jnp.int32)
        rows = lax.dynamic_slice_in_dim(quads, begin, rows_of_block, 0)
        gains = lax.dynamic_slice_in_dim(weight, begin, rows_of_block, 0)
        source = field[:, rows[:, 0], :] - field[:, rows[:, 1], :]
        receiver = field[:, rows[:, 2], :] - field[:, rows[:, 3], :]
        dots = source[0] * receiver[0] + source[1] * receiver[1] + source[2] * receiver[2]
        return (gains[:, None] * (-(volume[None, :] * dots))).astype(jnp.bfloat16)

    scaled_rows = lax.map(single_block, jnp.arange(MEASURE_TOTAL // rows_of_block).astype(jnp.int32))
    scaled_rows = scaled_rows.reshape(MEASURE_TOTAL, SLAB_CELLS).astype(jnp.float32)
    total_hessian = jnp.dot(scaled_rows.T, scaled_rows, precision=lax.Precision.HIGHEST, preferred_element_type=jnp.float32)
    return total_hessian / jnp.float32(MEASURE_TOTAL)
```

```python
import functools

import jax
import jax.numpy as jnp
from jax import lax
from jax.experimental import pallas as pl
from jax.experimental.pallas import tpu as pltpu
from jax.sharding import PartitionSpec as P

F32, BF16, I32 = jnp.float32, jnp.bfloat16, jnp.int32
TILES = 4
LIMIT = 24 * 1024 * 1024


def params():
    return pltpu.CompilerParams(vmem_limit_bytes=LIMIT)


def hop(x, axis, size, mask):
    return lax.ppermute(x, axis, [(i, i ^ mask) for i in range(size)])


def odd(d):
    return bin(d).count("1") % 2 == 1


def low_bit(d):
    return (d & -d).bit_length() - 1


def same_columns(left, right):
    return lax.dot_general(left, right, (((1,), (1,)), ((), ())), preferred_element_type=F32)


def difference_map(rows, at, base, depth):
    labels = lax.broadcasted_iota(jnp.int16, (depth, rows.shape[1]), 0)
    local = (rows - base).astype(jnp.int16)
    plus, minus = local[at : at + 1, :] == labels, local[at + 1 : at + 2, :] == labels
    one = jnp.ones((), BF16)
    return jnp.where(plus, one, jnp.where(minus, -one, jnp.zeros((), BF16)))


def turn(shards, turned, start=0):
    cells = shards[0].shape[2]
    for at, shard in enumerate(shards, start):
        for k in range(3):
            turned[at, k * cells : (k + 1) * cells, :] = shard[k].T


def turn_kernel(*refs):
    turn(refs[:-1], refs[-1])


def turn_shards(shards):
    _, depth, cells = shards[0].shape
    return pl.pallas_call(
        turn_kernel,
        out_shape=jax.ShapeDtypeStruct((len(shards), 3 * cells, depth), BF16),
        compiler_params=params(),
        cost_estimate=pl.CostEstimate(flops=1000, bytes_accessed=1000, transcendentals=0),
        name="turn_shards",
    )(*shards)


def sensitivity_kernel(ready, offsets, place, quads, weight, volume, *refs):
    shards, out, turned = refs[1 if ready else 0 : -2], refs[-2], refs[-1]
    cells, depth = out.shape[0], turned.shape[2]

    @pl.when(pl.program_id(0) == 0)
    def _():
        turn(shards, turned)

    rows = quads[...]
    source = receiver = None
    for at, offset in enumerate(offsets):
        base = jnp.bitwise_xor(place[0], offset) * depth
        left = refs[0][at] if at < ready else turned[at - ready]
        s = jnp.dot(left, difference_map(rows, 0, base, depth), preferred_element_type=F32)
        r = jnp.dot(left, difference_map(rows, 2, base, depth), preferred_element_type=F32)
        source = s if at == 0 else source + s
        receiver = r if at == 0 else receiver + r
    product = source * receiver
    dots = product[:cells] + product[cells : 2 * cells] + product[2 * cells :]
    out[...] = (weight[...] * -(volume[...] * dots)).astype(BF16)


def sensitivities(place, tiles, quads, weight, volume, shards, turned=None, ready=()):
    offsets = tuple(ready) + tuple(sorted(shards))
    held = [shards[k] for k in offsets[len(ready) :]]
    _, depth, cells = held[0].shape
    width = quads.shape[1] // TILES
    count = len(tiles)
    scalars = jnp.stack([place[0], *tiles]).astype(I32)
    spec = pltpu.PrefetchScalarGridSpec(
        num_scalar_prefetch=1,
        grid=(count,),
        in_specs=[
            pl.BlockSpec((4, width), lambda i, s: (0, s[1 + i])),
            pl.BlockSpec((1, width), lambda i, s: (0, s[1 + i])),
            pl.BlockSpec((cells, 1), lambda i, s: (0, 0)),
        ]
        + [pl.BlockSpec((len(ready), 3 * cells, depth), lambda i, s: (0, 0, 0))] * (1 if ready else 0)
        + [pl.BlockSpec((3, depth, cells), lambda i, s: (0, 0, 0))] * len(held),
        out_specs=pl.BlockSpec((cells, width), lambda i, s: (0, i)),
        scratch_shapes=[pltpu.VMEM((len(held), 3 * cells, depth), BF16)],
    )
    flops = 4 * count * width * len(offsets) * depth * 3 * cells
    return pl.pallas_call(
        functools.partial(sensitivity_kernel, len(ready), offsets),
        grid_spec=spec,
        out_shape=jax.ShapeDtypeStruct((cells, count * width), BF16),
        compiler_params=params(),
        cost_estimate=pl.CostEstimate(flops=flops, bytes_accessed=1, transcendentals=0),
        name="sensitivities",
    )(scalars, quads, weight, volume, *([turned] if ready else []), *held)


def pair_blocks(rows, own, other, core):
    return ((core, same_columns(rows, own)), (1 - core, same_columns(rows, other)))


def early_kernel(evens, place, own_send, own_keep, other_send, other_keep, *refs):
    recomputed, outs, every = refs[: len(evens)], refs[len(evens) : -1], refs[-1]
    core = place[2]
    sides = ((0, own_send, other_send), (1, own_keep, other_keep))

    def add(d, side, blocks):
        for column, block in blocks:
            if side == 0:
                every[d, column] = block
            else:
                every[d, column] += block

    for side, own, other in sides:
        add(0, side, pair_blocks(own[...], own[...], other[...], core))
    for at, d in enumerate(evens):
        part = own_send.shape[1] // 2
        for bit in range(2):

            @pl.when(jnp.bitwise_and(jnp.right_shift(place[1], low_bit(d)), 1) == bit)
            def _():
                lanes = slice(bit * part, (bit + 1) * part)
                for side, own, other in sides:
                    rows = recomputed[at][:, side * part : (side + 1) * part]
                    add(d, side, pair_blocks(rows, own[:, lanes], other[:, lanes], core))

    first = jnp.bitwise_xor(place[0], place[1])
    for k, out in enumerate(outs):
        out[...] = every[jnp.bitwise_xor(first, k)]


def late_kernel(odds, place, own_keep, other_keep, *refs):
    received, outs, every = refs[: len(odds)], refs[len(odds) : -1], refs[-1]
    for at, d in enumerate(odds):
        for column, block in pair_blocks(received[at][...], own_keep[...], other_keep[...], place[2]):
            every[d, column] = block
    first = jnp.bitwise_xor(place[0], place[1])
    for k, out in enumerate(outs):
        out[...] = every[jnp.bitwise_xor(first, k)]


def gather_kernel(width, place, own_early, own_late, *refs):
    received, mine, swap, mirror = refs[:-3], refs[-3], refs[-2], refs[-1]
    cells = own_early.shape[1]
    core = place[2]
    gap = jnp.bitwise_xor(place[0], place[1])
    late = functools.reduce(jnp.bitwise_xor, [jnp.bitwise_and(jnp.right_shift(gap, b), 1) for b in range(width)]) == 1

    def total(column):
        value = jnp.where(late, own_late[column], own_early[column])
        for part in received:
            value = value + part[column]
        return value

    mine[...] = total(core)
    swap[...] = total(1 - core).astype(BF16)
    for column in range(2):
        mirror[column * cells : (column + 1) * cells, :] = total(column).T.astype(BF16)


def final_kernel(amount, place, mine, swap, mirror, out):
    cells = mine.shape[0]
    core = place[2]
    here = pl.ds(pl.multiple_of(core * cells, cells), cells)
    there = pl.ds(pl.multiple_of((1 - core) * cells, cells), cells)
    out[here, :] = (mine[...] + mirror[here, :].astype(F32)) / amount
    out[there, :] = (swap[...].astype(F32) + mirror[there, :].astype(F32)) / amount


def whole_call(kernel, name, shapes, scratch, flops, place, *arrays):
    vmem = pl.BlockSpec(memory_space=pltpu.VMEM)
    many = isinstance(shapes, list)
    moved = sum(2 * a.size for a in arrays)
    return pl.pallas_call(
        kernel,
        in_specs=[pl.BlockSpec(memory_space=pltpu.SMEM)] + [vmem] * len(arrays),
        out_specs=[vmem] * len(shapes) if many else vmem,
        out_shape=shapes,
        scratch_shapes=scratch,
        compiler_params=params(),
        cost_estimate=pl.CostEstimate(flops=1, bytes_accessed=1, transcendentals=0),
        name=name,
    )(place, *arrays)


def to_group(x, k, late, groups, chips):
    pairs = [
        ((g * chips + p) * 2 + c, ((g ^ k) * chips + p) * 2 + c)
        for g in range(groups)
        for p in range(chips)
        for c in range(2)
        if odd(g ^ p ^ k) == late
    ]
    return lax.ppermute(x, ("elec", "cell"), pairs)


def per_device(grads, quads, volume, weight):
    groups, devices = lax.axis_size("elec"), lax.axis_size("cell")
    chips = devices // 2
    cells, measured = grads.shape[2], quads.shape[0]
    here = lax.axis_index("cell")
    group, chip, core = lax.axis_index("elec"), here // 2, here % 2
    place = jnp.stack([group, chip, core]).astype(I32)

    half, far = groups // 2, groups - 1
    shards = {0: grads, far: hop(grads, "elec", groups, far)}
    for j in range(1, half):
        shards[j] = hop(grads, "elec", groups, j)
    for j in range(1, half):
        shards[far ^ j] = hop(shards[far], "elec", groups, j)

    odds = [d for d in range(1, chips) if odd(d)]
    evens = [d for d in range(1, chips) if not odd(d)]
    columns, weights = quads.T, weight.reshape(1, measured)
    volumes = volume.reshape(cells, 1)
    volumes_across = {d: hop(volume, "cell", devices, 2 * d).reshape(cells, 1) for d in evens}
    bits = max(1, (chips - 1).bit_length())
    parity = functools.reduce(jnp.bitwise_xor, [(chip >> b) & 1 for b in range(bits)])
    keep, send = parity, 1 - parity
    keep_tiles, send_tiles = [2 * keep, 2 * keep + 1], [2 * send, 2 * send + 1]
    relayed = {far ^ j: shards[far ^ j] for j in range(1, half)}
    direct = {k: shards[k] for k in shards if k not in relayed}
    ready = tuple(sorted(direct))
    turned = turn_shards([direct[k] for k in ready])

    across = {}
    for d in evens:
        near, away = hop(grads, "cell", devices, 2 * d), hop(shards[far], "cell", devices, 2 * d)
        across[d] = {0: near, far: away}
        both = jnp.stack([near, away])
        both, relayed = lax.optimization_barrier((both, relayed))
        for j in range(1, half):
            moved = hop(both, "elec", groups, j)
            across[d][j], across[d][far ^ j] = moved[0], moved[1]

    form = functools.partial(sensitivities, place)
    own_send = form(send_tiles, columns, weights, volumes, relayed, turned, ready)
    received = [hop(own_send, "cell", devices, 2 * d) for d in odds]
    other_send = hop(own_send, "cell", devices, 1)
    columns, own_send = lax.optimization_barrier((columns, own_send))
    own_keep = form(keep_tiles, columns, weights, volumes, relayed, turned, ready)
    other_keep = hop(own_keep, "cell", devices, 1)
    recomputed = []
    for d in evens:
        bit = (chip >> low_bit(d)) & 1
        recomputed.append(form([2 * send + bit, 2 * keep + bit], columns, weights, volumes_across[d], across[d]))

    block = (2, cells, cells)
    shape = [jax.ShapeDtypeStruct(block, F32)] * groups
    every = [pltpu.VMEM((chips, *block), F32)]
    early = whole_call(
        functools.partial(early_kernel, evens), "early_blocks", shape, every, 1000,
        place, own_send, own_keep, other_send, other_keep, *recomputed,
    )
    late = whole_call(
        functools.partial(late_kernel, odds), "late_blocks", shape, every, 1000,
        place, own_keep, other_keep, *received,
    )
    arrived = [to_group(early[k], k, False, groups, chips) for k in range(1, groups)]
    arrived += [to_group(late[k], k, True, groups, chips) for k in range(1, groups)]
    mine, swap, mirror = whole_call(
        functools.partial(gather_kernel, bits),
        "sum_groups",
        [
            jax.ShapeDtypeStruct((cells, cells), F32),
            jax.ShapeDtypeStruct((cells, cells), BF16),
            jax.ShapeDtypeStruct((2 * cells, cells), BF16),
        ],
        [],
        1000,
        place, early[0], late[0], *arrived,
    )
    pairs = [
        (g * devices + 2 * p + c, p * devices + 2 * g + c)
        for g in range(groups)
        for p in range(chips)
        for c in range(2)
        if g != p
    ]
    mirrored = lax.ppermute(mirror, ("elec", "cell"), pairs)
    swapped = hop(swap, "cell", devices, 1)
    amount = float(measured * groups)
    return whole_call(
        functools.partial(final_kernel, amount),
        "finish",
        jax.ShapeDtypeStruct((2 * cells, cells), F32),
        [],
        1000,
        place, mine, swapped, mirrored,
    )


def solution(mesh):
    placed = (P(None, "elec", "cell"), P("elec", None), P("cell"), P("elec"))
    return jax.shard_map(
        per_device, mesh=mesh, in_specs=placed, out_specs=P("elec", "cell"), check_vma=False
    )
```

```python
import functools

import jax
import jax.numpy as jnp
from jax import lax
from jax.experimental import pallas as pl
from jax.experimental.pallas import tpu as pltpu
from jax.sharding import PartitionSpec as P

F32, BF16, I32 = jnp.float32, jnp.bfloat16, jnp.int32
TILES = 4
LIMIT = 24 * 1024 * 1024


def params():
    return pltpu.CompilerParams(vmem_limit_bytes=LIMIT)


def hop(x, axis, size, mask):
    return lax.ppermute(x, axis, [(i, i ^ mask) for i in range(size)])


def odd(d):
    return bin(d).count("1") % 2 == 1


def low_bit(d):
    return (d & -d).bit_length() - 1


def same_columns(left, right):
    return lax.dot_general(left, right, (((1,), (1,)), ((), ())), preferred_element_type=F32)


def difference_map(rows, at, base, depth):
    labels = lax.broadcasted_iota(jnp.int16, (depth, rows.shape[1]), 0)
    local = (rows - base).astype(jnp.int16)
    plus, minus = local[at : at + 1, :] == labels, local[at + 1 : at + 2, :] == labels
    one = jnp.ones((), BF16)
    return jnp.where(plus, one, jnp.where(minus, -one, jnp.zeros((), BF16)))


def turn(shards, turned, start=0):
    cells = shards[0].shape[2]
    for at, shard in enumerate(shards, start):
        for k in range(3):
            turned[at, k * cells : (k + 1) * cells, :] = shard[k].T


def turn_kernel(*refs):
    turn(refs[:-1], refs[-1])


def turn_shards(shards):
    _, depth, cells = shards[0].shape
    return pl.pallas_call(
        turn_kernel,
        out_shape=jax.ShapeDtypeStruct((len(shards), 3 * cells, depth), BF16),
        compiler_params=params(),
        cost_estimate=pl.CostEstimate(flops=1000, bytes_accessed=1000, transcendentals=0),
        name="turn_shards",
    )(*shards)


def sensitivity_kernel(ready, offsets, place, quads, weight, volume, *refs):
    shards, out, turned = refs[1 if ready else 0 : -2], refs[-2], refs[-1]
    cells, depth = out.shape[0], turned.shape[2]

    @pl.when(pl.program_id(0) == 0)
    def _():
        turn(shards, turned)

    rows = quads[...]
    source = receiver = None
    for at, offset in enumerate(offsets):
        base = jnp.bitwise_xor(place[0], offset) * depth
        left = refs[0][at] if at < ready else turned[at - ready]
        s = jnp.dot(left, difference_map(rows, 0, base, depth), preferred_element_type=F32)
        r = jnp.dot(left, difference_map(rows, 2, base, depth), preferred_element_type=F32)
        source = s if at == 0 else source + s
        receiver = r if at == 0 else receiver + r
    product = source * receiver
    dots = product[:cells] + product[cells : 2 * cells] + product[2 * cells :]
    out[...] = (weight[...] * -(volume[...] * dots)).astype(BF16)


def sensitivities(place, tiles, quads, weight, volume, shards, turned=None, ready=()):
    offsets = tuple(ready) + tuple(sorted(shards))
    held = [shards[k] for k in offsets[len(ready) :]]
    _, depth, cells = held[0].shape
    width = quads.shape[1] // TILES
    count = len(tiles)
    scalars = jnp.stack([place[0], *tiles]).astype(I32)
    spec = pltpu.PrefetchScalarGridSpec(
        num_scalar_prefetch=1,
        grid=(count,),
        in_specs=[
            pl.BlockSpec((4, width), lambda i, s: (0, s[1 + i])),
            pl.BlockSpec((1, width), lambda i, s: (0, s[1 + i])),
            pl.BlockSpec((cells, 1), lambda i, s: (0, 0)),
        ]
        + [pl.BlockSpec((len(ready), 3 * cells, depth), lambda i, s: (0, 0, 0))] * (1 if ready else 0)
        + [pl.BlockSpec((3, depth, cells), lambda i, s: (0, 0, 0))] * len(held),
        out_specs=pl.BlockSpec((cells, width), lambda i, s: (0, i)),
        scratch_shapes=[pltpu.VMEM((len(held), 3 * cells, depth), BF16)],
    )
    flops = 4 * count * width * len(offsets) * depth * 3 * cells
    return pl.pallas_call(
        functools.partial(sensitivity_kernel, len(ready), offsets),
        grid_spec=spec,
        out_shape=jax.ShapeDtypeStruct((cells, count * width), BF16),
        compiler_params=params(),
        cost_estimate=pl.CostEstimate(flops=flops, bytes_accessed=1, transcendentals=0),
        name="sensitivities",
    )(scalars, quads, weight, volume, *([turned] if ready else []), *held)


def pair_blocks(rows, own, other, core):
    return ((core, same_columns(rows, own)), (1 - core, same_columns(rows, other)))


def early_kernel(evens, place, own_send, own_keep, other_send, other_keep, *refs):
    recomputed, out = refs[: len(evens)], refs[-1]
    core = place[2]
    sides = ((0, own_send, other_send), (1, own_keep, other_keep))

    def add(at, side, blocks):
        for column, block in blocks:
            if side == 0:
                out[at, column] = block
            else:
                out[at, column] += block

    for side, own, other in sides:
        add(0, side, pair_blocks(own[...], own[...], other[...], core))
    for at, d in enumerate(evens):
        part = own_send.shape[1] // 2
        for bit in range(2):

            @pl.when(jnp.bitwise_and(jnp.right_shift(place[1], low_bit(d)), 1) == bit)
            def _():
                lanes = slice(bit * part, (bit + 1) * part)
                for side, own, other in sides:
                    rows = recomputed[at][:, side * part : (side + 1) * part]
                    add(1 + at, side, pair_blocks(rows, own[:, lanes], other[:, lanes], core))


def diagonal(cells):
    return lax.broadcasted_iota(I32, (cells, cells), 0) == lax.broadcasted_iota(I32, (cells, cells), 1)


def late_kernel(evens, odds, place, early, own_keep, other_keep, *refs):
    received, out_own, outs, every = refs[: len(odds)], refs[len(odds)], refs[len(odds) + 1 : -1], refs[-1]
    cells, core = early.shape[-1], place[2]
    every[0] = early[0]
    for at, d in enumerate(evens):
        every[d] = early[1 + at]
    for at, d in enumerate(odds):
        for column, block in pair_blocks(received[at][...], own_keep[...], other_keep[...], core):
            every[d, column] = block
    first = jnp.bitwise_xor(place[0], place[1])
    out_own[...] = every[first]
    for k, out in enumerate(outs, 1):
        d = jnp.bitwise_xor(first, k)
        for column in range(2):
            out[column * cells : (column + 1) * cells, :] = every[d, column].astype(BF16)
        square = every[d, core]
        lost = jnp.where(diagonal(cells), square - square.astype(BF16).astype(F32), 0.0)
        out[2 * cells :, :] = jnp.broadcast_to(jnp.sum(lost, axis=0, keepdims=True), (16, cells)).astype(BF16)


def gather_kernel(place, own, *refs):
    received, mine, swap, mirror = refs[:-3], refs[-3], refs[-2], refs[-1]
    cells = own.shape[1]
    core = place[2]

    def total(column):
        value = own[column]
        here = pl.ds(pl.multiple_of(column * cells, cells), cells)
        for part in received:
            value = value + part[here, :].astype(F32)
        lost = functools.reduce(jnp.add, [part[2 * cells : 2 * cells + 1, :].astype(F32) for part in received])
        return value + jnp.where(diagonal(cells) & (column == core), lost, 0.0)

    mine[...] = total(core)
    swap[...] = total(1 - core).astype(BF16)
    for column in range(2):
        mirror[column * cells : (column + 1) * cells, :] = total(column).T.astype(BF16)


def final_kernel(amount, place, mine, swap, mirror, out):
    cells = mine.shape[0]
    core = place[2]
    here = pl.ds(pl.multiple_of(core * cells, cells), cells)
    there = pl.ds(pl.multiple_of((1 - core) * cells, cells), cells)
    out[here, :] = (mine[...] + mirror[here, :].astype(F32)) / amount
    out[there, :] = (swap[...].astype(F32) + mirror[there, :].astype(F32)) / amount


def whole_call(kernel, name, shapes, scratch, flops, place, *arrays):
    vmem = pl.BlockSpec(memory_space=pltpu.VMEM)
    many = isinstance(shapes, list)
    moved = sum(2 * a.size for a in arrays)
    return pl.pallas_call(
        kernel,
        in_specs=[pl.BlockSpec(memory_space=pltpu.SMEM)] + [vmem] * len(arrays),
        out_specs=[vmem] * len(shapes) if many else vmem,
        out_shape=shapes,
        scratch_shapes=scratch,
        compiler_params=params(),
        cost_estimate=pl.CostEstimate(flops=1, bytes_accessed=1, transcendentals=0),
        name=name,
    )(place, *arrays)


def per_device(grads, quads, volume, weight):
    groups, devices = lax.axis_size("elec"), lax.axis_size("cell")
    chips = devices // 2
    cells, measured = grads.shape[2], quads.shape[0]
    here = lax.axis_index("cell")
    group, chip, core = lax.axis_index("elec"), here // 2, here % 2
    place = jnp.stack([group, chip, core]).astype(I32)

    half, far = groups // 2, groups - 1
    odds = [d for d in range(1, chips) if odd(d)]
    evens = [d for d in range(1, chips) if not odd(d)]
    shards = {far: hop(grads, "elec", groups, far)}
    volumes_across = {d: hop(volume, "cell", devices, 2 * d) for d in evens}
    shards[0], volumes_across = lax.optimization_barrier((grads, volumes_across))
    for j in range(1, half):
        shards[j] = hop(shards[0], "elec", groups, j)
    for j in range(1, half):
        shards[far ^ j] = hop(shards[far], "elec", groups, j)
    bits = max(1, (chips - 1).bit_length())
    parity = functools.reduce(jnp.bitwise_xor, [(chip >> b) & 1 for b in range(bits)])
    keep, send = parity, 1 - parity
    columns, weights = quads.T, weight.reshape(1, measured)
    volumes = volume.reshape(cells, 1)
    keep_tiles, send_tiles = [2 * keep, 2 * keep + 1], [2 * send, 2 * send + 1]
    relayed = {far ^ j: shards[far ^ j] for j in range(1, half)}
    direct = {k: shards[k] for k in shards if k not in relayed}
    ready = tuple(sorted(direct))
    turned = turn_shards([direct[k] for k in ready])

    across = {}
    for d in evens:
        near, away = hop(shards[0], "cell", devices, 2 * d), hop(shards[far], "cell", devices, 2 * d)
        across[d] = {0: near, far: away}
        both, relayed, turned = lax.optimization_barrier((jnp.stack([near, away]), relayed, turned))
        for j in range(1, half):
            moved = hop(both, "elec", groups, j)
            across[d][j], across[d][far ^ j] = moved[0], moved[1]

    form = functools.partial(sensitivities, place)
    own_send = form(send_tiles, columns, weights, volumes, relayed, turned, ready)
    received = [hop(own_send, "cell", devices, 2 * d) for d in odds]
    other_send = hop(own_send, "cell", devices, 1)
    columns, own_send = lax.optimization_barrier((columns, own_send))
    own_keep = form(keep_tiles, columns, weights, volumes, relayed, turned, ready)
    other_keep = hop(own_keep, "cell", devices, 1)
    recomputed = []
    for d in evens:
        bit = (chip >> low_bit(d)) & 1
        recomputed.append(form([2 * send + bit, 2 * keep + bit], columns, weights, volumes_across[d].reshape(cells, 1), across[d]))

    block = (2, cells, cells)
    early = whole_call(
        functools.partial(early_kernel, evens),
        "early_blocks",
        jax.ShapeDtypeStruct((1 + len(evens), *block), F32),
        [],
        1000,
        place, own_send, own_keep, other_send, other_keep, *recomputed,
    )
    parts = whole_call(
        functools.partial(late_kernel, evens, odds),
        "late_blocks",
        [jax.ShapeDtypeStruct(block, F32)] + [jax.ShapeDtypeStruct((2 * cells + 16, cells), BF16)] * (groups - 1),
        [pltpu.VMEM((chips, *block), F32)],
        1000,
        place, early, own_keep, other_keep, *received,
    )
    arrived = [hop(parts[k], "elec", groups, k) for k in range(1, groups)]
    mine, swap, mirror = whole_call(
        gather_kernel,
        "sum_groups",
        [
            jax.ShapeDtypeStruct((cells, cells), F32),
            jax.ShapeDtypeStruct((cells, cells), BF16),
            jax.ShapeDtypeStruct((2 * cells, cells), BF16),
        ],
        [],
        1000,
        place, parts[0], *arrived,
    )
    pairs = [
        (g * devices + 2 * p + c, p * devices + 2 * g + c)
        for g in range(groups)
        for p in range(chips)
        for c in range(2)
        if g != p
    ]
    mirrored = lax.ppermute(mirror, ("elec", "cell"), pairs)
    swapped = hop(swap, "cell", devices, 1)
    amount = float(measured * groups)
    return whole_call(
        functools.partial(final_kernel, amount),
        "finish",
        jax.ShapeDtypeStruct((2 * cells, cells), F32),
        [],
        1000,
        place, mine, swapped, mirrored,
    )


def solution(mesh):
    placed = (P(None, "elec", "cell"), P("elec", None), P("cell"), P("elec"))
    return jax.shard_map(
        per_device, mesh=mesh, in_specs=placed, out_specs=P("elec", "cell"), check_vma=False
    )
```

```python
import functools

import jax
import jax.numpy as jnp
from jax import lax
from jax.experimental import pallas as pl
from jax.experimental.pallas import tpu as pltpu
from jax.sharding import PartitionSpec as P

F32, BF16, I32 = jnp.float32, jnp.bfloat16, jnp.int32
TILES = 4
LIMIT = 24 * 1024 * 1024


def params():
    return pltpu.CompilerParams(vmem_limit_bytes=LIMIT)


def hop(x, axis, size, mask):
    return lax.ppermute(x, axis, [(i, i ^ mask) for i in range(size)])


def odd(d):
    return bin(d).count("1") % 2 == 1


def low_bit(d):
    return (d & -d).bit_length() - 1


def same_columns(left, right):
    return lax.dot_general(left, right, (((1,), (1,)), ((), ())), preferred_element_type=F32)


def difference_map(rows, at, base, depth):
    labels = lax.broadcasted_iota(jnp.int16, (depth, rows.shape[1]), 0)
    local = (rows - base).astype(jnp.int16)
    plus, minus = local[at : at + 1, :] == labels, local[at + 1 : at + 2, :] == labels
    one = jnp.ones((), BF16)
    return jnp.where(plus, one, jnp.where(minus, -one, jnp.zeros((), BF16)))


def turn(shards, turned, start=0):
    cells = shards[0].shape[2]
    for at, shard in enumerate(shards, start):
        for k in range(3):
            turned[at, k * cells : (k + 1) * cells, :] = shard[k].T


def turn_kernel(*refs):
    turn(refs[:-1], refs[-1])


def turn_shards(shards):
    _, depth, cells = shards[0].shape
    return pl.pallas_call(
        turn_kernel,
        out_shape=jax.ShapeDtypeStruct((len(shards), 3 * cells, depth), BF16),
        compiler_params=params(),
        cost_estimate=pl.CostEstimate(flops=1000, bytes_accessed=1000, transcendentals=0),
        name="turn_shards",
    )(*shards)


def pack_kernel(shard, volume, out):
    parts, depth, cells = shard.shape
    for k in range(parts):
        out[k * depth : (k + 1) * depth, :] = shard[k]
    rest = volume[...]
    rows = []
    for _ in range(3):
        rows.append(rest.astype(BF16).astype(F32))
        rest = rest - rows[-1]
    tail = jnp.concatenate(rows + [jnp.zeros((13, cells), F32)], axis=0)
    out[parts * depth :, :] = tail.astype(BF16)


def pack(shard, volume):
    parts, depth, cells = shard.shape
    return pl.pallas_call(
        pack_kernel,
        out_shape=jax.ShapeDtypeStruct((parts * depth + 16, cells), BF16),
        compiler_params=params(),
        cost_estimate=pl.CostEstimate(flops=1000, bytes_accessed=1000, transcendentals=0),
        name="pack",
    )(shard, volume.reshape(1, cells))


def sensitivity_kernel(ready, offsets, place, quads, weight, volume, *refs):
    shards, out, turned = refs[1 if ready else 0 : -2], refs[-2], refs[-1]
    cells, depth = out.shape[0], turned.shape[2]

    @pl.when(pl.program_id(0) == 0)
    def _():
        turn(shards, turned)

    rows = quads[...]
    source = receiver = None
    for at, offset in enumerate(offsets):
        base = jnp.bitwise_xor(place[0], offset) * depth
        left = refs[0][at] if at < ready else turned[at - ready]
        s = jnp.dot(left, difference_map(rows, 0, base, depth), preferred_element_type=F32)
        r = jnp.dot(left, difference_map(rows, 2, base, depth), preferred_element_type=F32)
        source = s if at == 0 else source + s
        receiver = r if at == 0 else receiver + r
    product = source * receiver
    dots = product[:cells] + product[cells : 2 * cells] + product[2 * cells :]
    terms = volume[...].astype(F32)
    column = jnp.sum(jnp.broadcast_to(terms[:, None, :], (terms.shape[0], 8, cells)), axis=0).T[:, :1]
    out[...] = (weight[...] * -(column * dots)).astype(BF16)


def sensitivities(place, tiles, quads, weight, volume, shards, turned=None, ready=()):
    offsets = tuple(ready) + tuple(sorted(shards))
    held = [shards[k] for k in offsets[len(ready) :]]
    _, depth, cells = held[0].shape
    width = quads.shape[1] // TILES
    count = len(tiles)
    scalars = jnp.stack([place[0], *tiles]).astype(I32)
    spec = pltpu.PrefetchScalarGridSpec(
        num_scalar_prefetch=1,
        grid=(count,),
        in_specs=[
            pl.BlockSpec((4, width), lambda i, s: (0, s[1 + i])),
            pl.BlockSpec((1, width), lambda i, s: (0, s[1 + i])),
            pl.BlockSpec(volume.shape, lambda i, s: (0, 0)),
        ]
        + [pl.BlockSpec((len(ready), 3 * cells, depth), lambda i, s: (0, 0, 0))] * (1 if ready else 0)
        + [pl.BlockSpec((3, depth, cells), lambda i, s: (0, 0, 0))] * len(held),
        out_specs=pl.BlockSpec((cells, width), lambda i, s: (0, i)),
        scratch_shapes=[pltpu.VMEM((len(held), 3 * cells, depth), BF16)],
    )
    flops = 4 * count * width * len(offsets) * depth * 3 * cells
    return pl.pallas_call(
        functools.partial(sensitivity_kernel, len(ready), offsets),
        grid_spec=spec,
        out_shape=jax.ShapeDtypeStruct((cells, count * width), BF16),
        compiler_params=params(),
        cost_estimate=pl.CostEstimate(flops=flops, bytes_accessed=1, transcendentals=0),
        name="sensitivities",
    )(scalars, quads, weight, volume, *([turned] if ready else []), *held)


def rows_of(core, cells):
    return pl.ds(pl.multiple_of(core * cells, cells), cells)


def early_kernel(evens, place, own_send, own_keep, other_send, other_keep, *refs):
    count, core = len(evens), place[2]
    recomputed, own_block, mine, swap = refs[:count], *refs[count : count + 3]
    mirrors, pair = refs[count + 3 : -1], refs[-1]
    cells = own_send.shape[0]
    here, there = rows_of(core, cells), rows_of(1 - core, cells)
    sides = ((0, own_send, other_send), (1, own_keep, other_keep))
    own_block[here, :] = functools.reduce(jnp.add, [same_columns(own[...], own[...]) for _, own, _ in sides])
    own_block[there, :] = functools.reduce(jnp.add, [same_columns(other[...], own[...]) for _, own, other in sides])
    for at, d in enumerate(evens):
        part = own_send.shape[1] // 2
        for bit in range(2):

            @pl.when(jnp.bitwise_and(jnp.right_shift(place[1], low_bit(d)), 1) == bit)
            def _():
                lanes = slice(bit * part, (bit + 1) * part)
                for side, own, other in sides:
                    rows = recomputed[at][:, side * part : (side + 1) * part]
                    for which, columns in enumerate((own, other)):
                        block = same_columns(rows, columns[:, lanes])
                        pair[which] = block if side == 0 else pair[which] + block

        mine[at] = pair[0]
        swap[at] = pair[1].astype(BF16)
        mirrors[at][here, :] = pair[0].T.astype(BF16)
        mirrors[at][there, :] = pair[1].T.astype(BF16)


def late_kernel(odds, place, own_keep, other_keep, *refs):
    count, core = len(odds), place[2]
    received, mine, swap, mirrors = refs[:count], refs[count], refs[count + 1], refs[count + 2 :]
    cells = own_keep.shape[0]
    here, there = rows_of(core, cells), rows_of(1 - core, cells)
    for at in range(count):
        rows = received[at][...]
        block, across = same_columns(rows, own_keep[...]), same_columns(rows, other_keep[...])
        mine[at] = block
        swap[at] = across.astype(BF16)
        mirrors[at][here, :] = block.T.astype(BF16)
        mirrors[at][there, :] = across.T.astype(BF16)


def diagonal(cells):
    return lax.broadcasted_iota(I32, (cells, cells), 0) == lax.broadcasted_iota(I32, (cells, cells), 1)


def combine_kernel(evens, odds, place, own_block, *refs):
    core, every = place[2], refs[-1]
    cells = own_block.shape[1]
    here, there = rows_of(core, cells), rows_of(1 - core, cells)
    every[0] = own_block[...]
    at = 0
    for group in (evens, odds):
        mine, swapped, mirrored = refs[at], refs[at + 1], refs[at + 2 : at + 2 + len(group)]
        at += 2 + len(group)
        for i, d in enumerate(group):
            every[d, here, :] = mine[i] + mirrored[i][here, :].astype(F32)
            every[d, there, :] = swapped[i].astype(F32) + mirrored[i][there, :].astype(F32)
    out_own, outs = refs[at], refs[at + 1 : -1]
    first = jnp.bitwise_xor(place[0], place[1])
    out_own[...] = every[first]
    for k, out in enumerate(outs, 1):
        d = jnp.bitwise_xor(first, k)
        out[: 2 * cells, :] = every[d].astype(BF16)
        square = every[d, here, :]
        lost = jnp.where(diagonal(cells), square - square.astype(BF16).astype(F32), 0.0)
        out[2 * cells :, :] = jnp.broadcast_to(jnp.sum(lost, axis=0, keepdims=True), (16, cells)).astype(BF16)


def final_kernel(amount, place, own, *refs):
    received, out = refs[:-1], refs[-1]
    cells = own.shape[1]
    total = own[...]
    for part in received:
        total = total + part[: 2 * cells, :].astype(F32)
    out[...] = total / amount
    lost = functools.reduce(jnp.add, [part[2 * cells : 2 * cells + 1, :].astype(F32) for part in received])
    here = rows_of(place[2], cells)
    out[here, :] += jnp.where(diagonal(cells), lost / amount, 0.0)


def whole_call(kernel, name, shapes, scratch, place, *arrays):
    vmem = pl.BlockSpec(memory_space=pltpu.VMEM)
    many = isinstance(shapes, list)
    return pl.pallas_call(
        kernel,
        in_specs=[pl.BlockSpec(memory_space=pltpu.SMEM)] + [vmem] * len(arrays),
        out_specs=[vmem] * len(shapes) if many else vmem,
        out_shape=shapes,
        scratch_shapes=scratch,
        compiler_params=params(),
        cost_estimate=pl.CostEstimate(flops=1, bytes_accessed=1, transcendentals=0),
        name=name,
    )(place, *arrays)


def per_device(grads, quads, volume, weight):
    groups, devices = lax.axis_size("elec"), lax.axis_size("cell")
    chips = devices // 2
    cells, measured = grads.shape[2], quads.shape[0]
    here = lax.axis_index("cell")
    group, chip, core = lax.axis_index("elec"), here // 2, here % 2
    place = jnp.stack([group, chip, core]).astype(I32)

    half, far = groups // 2, groups - 1
    odds = [d for d in range(1, chips) if odd(d)]
    evens = [d for d in range(1, chips) if not odd(d)]
    packed = pack(grads, volume)
    shape = grads.shape
    gradients = lambda x: x[: 3 * shape[1], :].reshape(shape)
    shards = {0: grads, far: hop(grads, "elec", groups, far)}
    for j in range(1, half):
        shards[j] = gradients(hop(packed, "elec", groups, j))
    for j in range(1, half):
        shards[far ^ j] = hop(shards[far], "elec", groups, j)

    bits = max(1, (chips - 1).bit_length())
    parity = functools.reduce(jnp.bitwise_xor, [(chip >> b) & 1 for b in range(bits)])
    keep, send = parity, 1 - parity
    columns, weights = quads.T, weight.reshape(1, measured)
    volumes = volume.reshape(1, cells)
    keep_tiles, send_tiles = [2 * keep, 2 * keep + 1], [2 * send, 2 * send + 1]
    relayed = {far ^ j: shards[far ^ j] for j in range(1, half)}
    direct = {k: shards[k] for k in shards if k not in relayed}
    ready = tuple(sorted(direct))
    turned = turn_shards([direct[k] for k in ready])

    across, volumes_across = {}, {}
    for d in evens:
        near, away = hop(packed, "cell", devices, 2 * d), hop(shards[far], "cell", devices, 2 * d)
        near, volumes_across[d] = gradients(near), near[3 * shape[1] :, :]
        across[d] = {0: near, far: away}
        both, relayed, turned = lax.optimization_barrier((jnp.stack([near, away]), relayed, turned))
        for j in range(1, half):
            moved = hop(both, "elec", groups, j)
            across[d][j], across[d][far ^ j] = moved[0], moved[1]

    form = functools.partial(sensitivities, place)
    own_send = form(send_tiles, columns, weights, volumes, relayed, turned, ready)
    received = [hop(own_send, "cell", devices, 2 * d) for d in odds]
    other_send = hop(own_send, "cell", devices, 1)
    columns, own_send = lax.optimization_barrier((columns, own_send))
    own_keep = form(keep_tiles, columns, weights, volumes, relayed, turned, ready)
    other_keep = hop(own_keep, "cell", devices, 1)
    recomputed = []
    for d in evens:
        bit = (chip >> low_bit(d)) & 1
        recomputed.append(form([2 * send + bit, 2 * keep + bit], columns, weights, volumes_across[d], across[d]))

    whole, small = (2 * cells, cells), (cells, cells)
    outputs = lambda group: [
        jax.ShapeDtypeStruct((len(group), *small), F32),
        jax.ShapeDtypeStruct((len(group), *small), BF16),
    ] + [jax.ShapeDtypeStruct(whole, BF16)] * len(group)
    own_block, *early = whole_call(
        functools.partial(early_kernel, evens),
        "early_blocks",
        [jax.ShapeDtypeStruct(whole, F32)] + outputs(evens),
        [pltpu.VMEM((2, *small), F32)],
        place, own_send, own_keep, other_send, other_keep, *recomputed,
    )
    late = whole_call(functools.partial(late_kernel, odds), "late_blocks", outputs(odds), [], place, own_keep, other_keep, *received)

    def exchange(group, mine, swap, *mirrors):
        moved = [hop(m, "cell", devices, 2 * d) for d, m in zip(group, mirrors)]
        return [mine, hop(swap, "cell", devices, 1)] + moved

    parts = whole_call(
        functools.partial(combine_kernel, evens, odds),
        "combine",
        [jax.ShapeDtypeStruct(whole, F32)] + [jax.ShapeDtypeStruct((2 * cells + 16, cells), BF16)] * (groups - 1),
        [pltpu.VMEM((chips, *whole), F32)],
        place, own_block, *exchange(evens, *early), *exchange(odds, *late),
    )
    arrived = [hop(parts[k], "elec", groups, k) for k in range(1, groups)]
    return whole_call(
        functools.partial(final_kernel, float(measured * groups)),
        "finish",
        jax.ShapeDtypeStruct(whole, F32),
        [],
        place, parts[0], *arrived,
    )


def solution(mesh):
    placed = (P(None, "elec", "cell"), P("elec", None), P("cell"), P("elec"))
    return jax.shard_map(
        per_device, mesh=mesh, in_specs=placed, out_specs=P("elec", "cell"), check_vma=False
    )
```

```python
import functools

import jax
import jax.numpy as jnp
from jax import lax
from jax.experimental import pallas as pl
from jax.experimental.pallas import tpu as pltpu
from jax.sharding import PartitionSpec as P

F32, BF16, I32 = jnp.float32, jnp.bfloat16, jnp.int32
WEIGH = 4
TILES = 4
LIMIT = 24 * 1024 * 1024


def params():
    return pltpu.CompilerParams(vmem_limit_bytes=LIMIT)


def hop(x, axis, size, mask):
    return lax.ppermute(x, axis, [(i, i ^ mask) for i in range(size)])


def odd(d):
    return bin(d).count("1") % 2 == 1


def low_bit(d):
    return (d & -d).bit_length() - 1


def difference_map(places, at, total):
    labels = lax.broadcasted_iota(jnp.int16, (total, places.shape[1]), 0)
    plus, minus = places[at : at + 1, :] == labels, places[at + 1 : at + 2, :] == labels
    one = jnp.ones((), BF16)
    return jnp.where(plus, one, jnp.where(minus, -one, jnp.zeros((), BF16)))


def turn(shards, turned, start=0):
    _, depth, cells = shards[0].shape
    for at, shard in enumerate(shards, start):
        for k in range(3):
            turned[k * cells : (k + 1) * cells, at * depth : (at + 1) * depth] = shard[k].T


def turn_kernel(*refs):
    turn(refs[:-1], refs[-1])


def turn_shards(shards):
    _, depth, cells = shards[0].shape
    return pl.pallas_call(
        turn_kernel,
        out_shape=jax.ShapeDtypeStruct((3 * cells, len(shards) * depth), BF16),
        compiler_params=params(),
        cost_estimate=pl.CostEstimate(flops=1000, bytes_accessed=1000, transcendentals=0),
        name="turn_shards",
    )(*shards)


def pack_kernel(shard, volume, out):
    parts, depth, cells = shard.shape
    for k in range(parts):
        out[k * depth : (k + 1) * depth, :] = shard[k]
    rest = volume[...]
    rows = []
    for _ in range(3):
        rows.append(rest.astype(BF16).astype(F32))
        rest = rest - rows[-1]
    tail = jnp.concatenate(rows + [jnp.zeros((13, cells), F32)], axis=0)
    out[parts * depth :, :] = tail.astype(BF16)


def pack(shard, volume):
    parts, depth, cells = shard.shape
    return pl.pallas_call(
        pack_kernel,
        out_shape=jax.ShapeDtypeStruct((parts * depth + 16, cells), BF16),
        compiler_params=params(),
        cost_estimate=pl.CostEstimate(flops=1000, bytes_accessed=1000, transcendentals=0),
        name="pack",
    )(shard, volume.reshape(1, cells))


def sensitivity_kernel(offsets, ready, count, place, *refs):
    quads, weights, volume = refs[:count], refs[count : 2 * count], refs[2 * count]
    shards, out, turned = refs[2 * count + (2 if ready else 1) : -2], refs[-2], refs[-1]
    cells, width = out.shape[0], quads[0].shape[1]
    depth = turned.shape[1] // len(offsets)
    if ready:
        turned[:, : ready * depth] = refs[2 * count + 1][...]
    turn(shards, turned, ready)
    terms = volume[...].astype(F32)
    column = jnp.sum(jnp.broadcast_to(terms[:, None, :], (terms.shape[0], 8, cells)), axis=0).T[:, :1]
    for tile in range(count):
        rows = quads[tile][...]
        owner = rows // depth
        slot = jnp.bitwise_xor(owner, place[0])
        if offsets != tuple(range(len(offsets))):
            slot = functools.reduce(jnp.add, [jnp.where(slot == k, at, 0) for at, k in enumerate(offsets)])
        places = (slot * depth + (rows - owner * depth)).astype(jnp.int16)
        source = jnp.dot(turned[...], difference_map(places, 0, turned.shape[1]), preferred_element_type=F32)
        receiver = jnp.dot(turned[...], difference_map(places, 2, turned.shape[1]), preferred_element_type=F32)
        product = source * receiver
        dots = product[:cells] + product[cells : 2 * cells] + product[2 * cells :]
        out[:, tile * width : (tile + 1) * width] = (weights[tile][...] * -(column * dots)).astype(BF16)


def sensitivities(place, tiles, quads, weight, volume, shards, turned=None, ready=(), weigh=1):
    offsets = tuple(ready) + tuple(sorted(shards))
    held = [shards[k] for k in offsets[len(ready) :]]
    _, depth, cells = held[0].shape
    width = quads.shape[1] // TILES
    count = len(tiles)
    scalars = jnp.stack([place[0], *tiles]).astype(I32)
    whole = lambda a: pl.BlockSpec(a.shape, lambda i, s: (0,) * a.ndim)
    tile_of = lambda rows, t: pl.BlockSpec((rows, width), lambda i, s: (0, s[1 + t]))
    rest = [volume] + ([turned] if ready else []) + held
    spec = pltpu.PrefetchScalarGridSpec(
        num_scalar_prefetch=1,
        grid=(1,),
        in_specs=[tile_of(4, t) for t in range(count)] + [tile_of(1, t) for t in range(count)] + [whole(a) for a in rest],
        out_specs=pl.BlockSpec((cells, count * width), lambda i, s: (0, 0)),
        scratch_shapes=[pltpu.VMEM((3 * cells, len(offsets) * depth), BF16)],
    )
    flops = weigh * 4 * count * width * len(offsets) * depth * 3 * cells
    return pl.pallas_call(
        functools.partial(sensitivity_kernel, offsets, len(ready), count),
        grid_spec=spec,
        out_shape=jax.ShapeDtypeStruct((cells, count * width), BF16),
        compiler_params=params(),
        cost_estimate=pl.CostEstimate(flops=flops, bytes_accessed=1, transcendentals=0),
        name="sensitivities",
    )(scalars, *[quads] * count, *[weight] * count, *rest)


def same_columns(left, right):
    return lax.dot_general(left, right, (((1,), (1,)), ((), ())), preferred_element_type=F32)


def rows_of(core, cells):
    return pl.ds(pl.multiple_of(core * cells, cells), cells)


def early_kernel(evens, place, own_send, own_keep, other_send, other_keep, *refs):
    count, core = len(evens), place[2]
    recomputed, mine, swap = refs[:count], *refs[count : count + 2]
    mirrors, pair = refs[count + 2 : -1], refs[-1]
    cells = own_send.shape[0]
    here, there = rows_of(core, cells), rows_of(1 - core, cells)
    sides = ((0, own_send, other_send), (1, own_keep, other_keep))
    for at, d in enumerate(evens):
        part = own_send.shape[1] // 2
        for bit in range(2):

            @pl.when(jnp.bitwise_and(jnp.right_shift(place[1], low_bit(d)), 1) == bit)
            def _():
                lanes = slice(bit * part, (bit + 1) * part)
                for side, own, other in sides:
                    rows = recomputed[at][:, side * part : (side + 1) * part]
                    for which, columns in enumerate((own, other)):
                        block = same_columns(rows, columns[:, lanes])
                        pair[which] = block if side == 0 else pair[which] + block

        mine[at] = pair[0]
        swap[at] = pair[1].astype(BF16)
        mirrors[at][here, :] = pair[0].T.astype(BF16)
        mirrors[at][there, :] = pair[1].T.astype(BF16)


def own_kernel(place, own_send, own_keep, other_send, other_keep, out):
    cells = own_send.shape[0]
    sides = ((own_send[...], other_send[...]), (own_keep[...], other_keep[...]))
    out[rows_of(place[2], cells), :] = functools.reduce(jnp.add, [same_columns(own, own) for own, _ in sides])
    out[rows_of(1 - place[2], cells), :] = functools.reduce(jnp.add, [same_columns(other, own) for own, other in sides])


def late_kernel(odds, place, own_keep, other_keep, *refs):
    count, core = len(odds), place[2]
    received, mine, swap, mirrors = refs[:count], refs[count], refs[count + 1], refs[count + 2 :]
    cells = own_keep.shape[0]
    here, there = rows_of(core, cells), rows_of(1 - core, cells)
    for at in range(count):
        rows = received[at][...]
        block, across = same_columns(rows, own_keep[...]), same_columns(rows, other_keep[...])
        mine[at] = block
        swap[at] = across.astype(BF16)
        mirrors[at][here, :] = block.T.astype(BF16)
        mirrors[at][there, :] = across.T.astype(BF16)


def diagonal(cells):
    return lax.broadcasted_iota(I32, (cells, cells), 0) == lax.broadcasted_iota(I32, (cells, cells), 1)


def combine_kernel(evens, odds, place, own_block, *refs):
    core, every = place[2], refs[-1]
    cells = own_block.shape[1]
    here, there = rows_of(core, cells), rows_of(1 - core, cells)
    every[0] = own_block[...]
    at = 0
    for group in (evens, odds):
        mine, swapped, mirrored = refs[at], refs[at + 1], refs[at + 2 : at + 2 + len(group)]
        at += 2 + len(group)
        for i, d in enumerate(group):
            every[d, here, :] = mine[i] + mirrored[i][here, :].astype(F32)
            every[d, there, :] = swapped[i].astype(F32) + mirrored[i][there, :].astype(F32)
    out_own, outs = refs[at], refs[at + 1 : -1]
    first = jnp.bitwise_xor(place[0], place[1])
    out_own[...] = every[first]
    for k, out in enumerate(outs, 1):
        d = jnp.bitwise_xor(first, k)
        out[: 2 * cells, :] = every[d].astype(BF16)
        square = every[d, here, :]
        lost = jnp.where(diagonal(cells), square - square.astype(BF16).astype(F32), 0.0)
        out[2 * cells :, :] = jnp.broadcast_to(jnp.sum(lost, axis=0, keepdims=True), (16, cells)).astype(BF16)


def final_kernel(amount, place, own, *refs):
    received, out = refs[:-1], refs[-1]
    cells = own.shape[1]
    total = own[...]
    for part in received:
        total = total + part[: 2 * cells, :].astype(F32)
    out[...] = total / amount
    lost = functools.reduce(jnp.add, [part[2 * cells : 2 * cells + 1, :].astype(F32) for part in received])
    here = rows_of(place[2], cells)
    out[here, :] += jnp.where(diagonal(cells), lost / amount, 0.0)


def whole_call(kernel, name, shapes, scratch, place, *arrays):
    vmem = pl.BlockSpec(memory_space=pltpu.VMEM)
    many = isinstance(shapes, list)
    return pl.pallas_call(
        kernel,
        in_specs=[pl.BlockSpec(memory_space=pltpu.SMEM)] + [vmem] * len(arrays),
        out_specs=[vmem] * len(shapes) if many else vmem,
        out_shape=shapes,
        scratch_shapes=scratch,
        compiler_params=params(),
        cost_estimate=pl.CostEstimate(flops=1, bytes_accessed=1, transcendentals=0),
        name=name,
    )(place, *arrays)


def per_device(grads, quads, volume, weight):
    groups, devices = lax.axis_size("elec"), lax.axis_size("cell")
    chips = devices // 2
    cells, measured = grads.shape[2], quads.shape[0]
    here = lax.axis_index("cell")
    group, chip, core = lax.axis_index("elec"), here // 2, here % 2
    place = jnp.stack([group, chip, core]).astype(I32)

    half, far = groups // 2, groups - 1
    odds = [d for d in range(1, chips) if odd(d)]
    evens = [d for d in range(1, chips) if not odd(d)]
    packed = pack(grads, volume)
    shape = grads.shape
    gradients = lambda x: x[: 3 * shape[1], :].reshape(shape)
    shards = {0: grads, far: hop(grads, "elec", groups, far)}
    for j in range(1, half):
        shards[j] = gradients(hop(packed, "elec", groups, j))
    for j in range(1, half):
        shards[far ^ j] = hop(shards[far], "elec", groups, j)

    bits = max(1, (chips - 1).bit_length())
    parity = functools.reduce(jnp.bitwise_xor, [(chip >> b) & 1 for b in range(bits)])
    keep, send = parity, 1 - parity
    columns, weights = quads.T, weight.reshape(1, measured)
    volumes = volume.reshape(1, cells)
    keep_tiles, send_tiles = [2 * keep, 2 * keep + 1], [2 * send, 2 * send + 1]
    relayed = {far ^ j: shards[far ^ j] for j in range(1, half)}
    direct = {k: shards[k] for k in shards if k not in relayed}
    ready = tuple(sorted(direct))
    turned = turn_shards([direct[k] for k in ready])

    across, volumes_across = {}, {}
    for d in evens:
        near = hop(packed, "cell", devices, 2 * d)
        near, volumes_across[d] = gradients(near), near[3 * shape[1] :, :]
        across[d] = {0: near}
        for k in [far, *range(1, half)]:
            across[d][k] = hop(shards[k], "cell", devices, 2 * d)

    form = functools.partial(sensitivities, place)
    own_send = form(send_tiles, columns, weights, volumes, relayed, turned, ready)
    received = [hop(own_send, "cell", devices, 2 * d) for d in odds]
    other_send = hop(own_send, "cell", devices, 1)
    columns, own_send, across = lax.optimization_barrier((columns, own_send, across))
    for d in evens:
        for j in range(1, half):
            across[d][far ^ j] = hop(across[d][far], "elec", groups, j)
    own_keep = form(keep_tiles, columns, weights, volumes, relayed, turned, ready)
    other_keep = hop(own_keep, "cell", devices, 1)
    recomputed = []
    for d in evens:
        bit = (chip >> low_bit(d)) & 1
        recomputed.append(form([2 * send + bit, 2 * keep + bit], columns, weights, volumes_across[d], across[d], weigh=WEIGH))

    whole, small = (2 * cells, cells), (cells, cells)
    outputs = lambda group: [
        jax.ShapeDtypeStruct((len(group), *small), F32),
        jax.ShapeDtypeStruct((len(group), *small), BF16),
    ] + [jax.ShapeDtypeStruct(whole, BF16)] * len(group)
    early = whole_call(
        functools.partial(early_kernel, evens),
        "early_blocks",
        outputs(evens),
        [pltpu.VMEM((2, *small), F32)],
        place, own_send, own_keep, other_send, other_keep, *recomputed,
    )
    late = whole_call(functools.partial(late_kernel, odds), "late_blocks", outputs(odds), [], place, own_keep, other_keep, *received)

    own_keep, late = lax.optimization_barrier((own_keep, late))
    own_block = whole_call(
        own_kernel, "own_block", jax.ShapeDtypeStruct(whole, F32), [], place, own_send, own_keep, other_send, other_keep
    )

    def exchange(group, mine, swap, *mirrors):
        moved = [hop(m, "cell", devices, 2 * d) for d, m in zip(group, mirrors)]
        return [mine, hop(swap, "cell", devices, 1)] + moved

    parts = whole_call(
        functools.partial(combine_kernel, evens, odds),
        "combine",
        [jax.ShapeDtypeStruct(whole, F32)] + [jax.ShapeDtypeStruct((2 * cells + 16, cells), BF16)] * (groups - 1),
        [pltpu.VMEM((chips, *whole), F32)],
        place, own_block, *exchange(evens, *early), *exchange(odds, *late),
    )
    arrived = [hop(parts[k], "elec", groups, k) for k in reversed(range(1, groups))]
    return whole_call(
        functools.partial(final_kernel, float(measured * groups)),
        "finish",
        jax.ShapeDtypeStruct(whole, F32),
        [],
        place, parts[0], *arrived,
    )


def solution(mesh):
    placed = (P(None, "elec", "cell"), P("elec", None), P("cell"), P("elec"))
    return jax.shard_map(
        per_device, mesh=mesh, in_specs=placed, out_specs=P("elec", "cell"), check_vma=False
    )
```

```python
import functools

import jax
import jax.numpy as jnp
from jax import lax
from jax.experimental import pallas as pl
from jax.experimental.pallas import tpu as pltpu
from jax.sharding import PartitionSpec as P

F32, BF16, I32 = jnp.float32, jnp.bfloat16, jnp.int32
WEIGH = 4
TILES = 4
LIMIT = 24 * 1024 * 1024


def params():
    return pltpu.CompilerParams(vmem_limit_bytes=LIMIT)


def hop(x, axis, size, mask):
    return lax.ppermute(x, axis, [(i, i ^ mask) for i in range(size)])


def odd(d):
    return bin(d).count("1") % 2 == 1


def position():
    here = lax.axis_index("cell")
    return lax.axis_index("elec"), jnp.right_shift(here, 1), jnp.bitwise_and(here, 1)


def bit_of(number, at):
    return jnp.bitwise_and(jnp.right_shift(number, at), 1)


def tiles_of(which, bits):
    _, chip, _ = position()
    keep = functools.reduce(jnp.bitwise_xor, [bit_of(chip, b) for b in range(bits)])
    send = 1 - keep
    if which == "send":
        return 2 * send, 2 * send + 1
    if which == "keep":
        return 2 * keep, 2 * keep + 1
    bit = bit_of(chip, low_bit(which))
    return 2 * send + bit, 2 * keep + bit


def low_bit(d):
    return (d & -d).bit_length() - 1


def difference_map(places, at, total):
    labels = lax.broadcasted_iota(jnp.int16, (total, places.shape[1]), 0)
    plus, minus = places[at : at + 1, :] == labels, places[at + 1 : at + 2, :] == labels
    one = jnp.ones((), BF16)
    return jnp.where(plus, one, jnp.where(minus, -one, jnp.zeros((), BF16)))


def turn(shards, turned, start=0):
    _, depth, cells = shards[0].shape
    for at, shard in enumerate(shards, start):
        for k in range(3):
            turned[k * cells : (k + 1) * cells, at * depth : (at + 1) * depth] = shard[k].T


def turn_kernel(*refs):
    turn(refs[:-1], refs[-1])


def turn_shards(shards):
    _, depth, cells = shards[0].shape
    return pl.pallas_call(
        turn_kernel,
        out_shape=jax.ShapeDtypeStruct((3 * cells, len(shards) * depth), BF16),
        compiler_params=params(),
        cost_estimate=pl.CostEstimate(flops=1000, bytes_accessed=1000, transcendentals=0),
        name="turn_shards",
    )(*shards)


def pack_kernel(shard, volume, out):
    parts, depth, cells = shard.shape
    for k in range(parts):
        out[k * depth : (k + 1) * depth, :] = shard[k]
    rest = volume[...]
    rows = []
    for _ in range(3):
        rows.append(rest.astype(BF16).astype(F32))
        rest = rest - rows[-1]
    tail = jnp.concatenate(rows + [jnp.zeros((13, cells), F32)], axis=0)
    out[parts * depth :, :] = tail.astype(BF16)


def pack(shard, volume):
    parts, depth, cells = shard.shape
    return pl.pallas_call(
        pack_kernel,
        out_shape=jax.ShapeDtypeStruct((parts * depth + 16, cells), BF16),
        compiler_params=params(),
        cost_estimate=pl.CostEstimate(flops=1000, bytes_accessed=1000, transcendentals=0),
        name="pack",
    )(shard, volume.reshape(1, cells))


def sensitivity_kernel(offsets, ready, which, bits, quads, weight, volume, *refs):
    shards, out, turned = refs[1 if ready else 0 : -2], refs[-2], refs[-1]
    cells, width = out.shape[0], quads.shape[1] // TILES
    depth = turned.shape[1] // len(offsets)
    if ready:
        turned[:, : ready * depth] = refs[0][...]
    turn(shards, turned, ready)
    terms = volume[...].astype(F32)
    column = jnp.sum(jnp.broadcast_to(terms[:, None, :], (terms.shape[0], 8, cells)), axis=0).T[:, :1]
    group, _, _ = position()
    for at, tile in enumerate(tiles_of(which, bits)):
        lanes = pl.ds(pl.multiple_of(tile * width, width), width)
        rows = quads[:, lanes]
        owner = rows // depth
        slot = jnp.bitwise_xor(owner, group)
        if offsets != tuple(range(len(offsets))):
            slot = functools.reduce(jnp.add, [jnp.where(slot == k, n, 0) for n, k in enumerate(offsets)])
        places = (slot * depth + (rows - owner * depth)).astype(jnp.int16)
        source = jnp.dot(turned[...], difference_map(places, 0, turned.shape[1]), preferred_element_type=F32)
        receiver = jnp.dot(turned[...], difference_map(places, 2, turned.shape[1]), preferred_element_type=F32)
        product = source * receiver
        dots = product[:cells] + product[cells : 2 * cells] + product[2 * cells :]
        out[:, at * width : (at + 1) * width] = (weight[:, lanes] * -(column * dots)).astype(BF16)


def sensitivities(which, bits, quads, weight, volume, shards, turned=None, ready=(), weigh=1):
    offsets = tuple(ready) + tuple(sorted(shards))
    held = [shards[k] for k in offsets[len(ready) :]]
    _, depth, cells = held[0].shape
    count, width = 2, quads.shape[1] // TILES
    flops = weigh * 4 * count * width * len(offsets) * depth * 3 * cells
    return whole_call(
        functools.partial(sensitivity_kernel, offsets, len(ready), which, bits),
        "sensitivities",
        jax.ShapeDtypeStruct((cells, count * width), BF16),
        [pltpu.VMEM((3 * cells, len(offsets) * depth), BF16)],
        quads, weight, volume, *([turned] if ready else []), *held,
        flops=flops,
    )


def same_columns(left, right):
    return lax.dot_general(left, right, (((1,), (1,)), ((), ())), preferred_element_type=F32)


def rows_of(core, cells):
    return pl.ds(pl.multiple_of(core * cells, cells), cells)


def early_kernel(evens, own_send, own_keep, other_send, other_keep, *refs):
    count, (_, chip, core) = len(evens), position()
    recomputed, mine, swap = refs[:count], *refs[count : count + 2]
    mirrors, pair = refs[count + 2 : -1], refs[-1]
    cells = own_send.shape[0]
    here, there = rows_of(core, cells), rows_of(1 - core, cells)
    sides = ((0, own_send, other_send), (1, own_keep, other_keep))
    for at, d in enumerate(evens):
        part = own_send.shape[1] // 2
        for bit in range(2):

            @pl.when(bit_of(chip, low_bit(d)) == bit)
            def _():
                lanes = slice(bit * part, (bit + 1) * part)
                columns = [jnp.concatenate([own[:, lanes], other[:, lanes]], axis=0) for _, own, other in sides]
                blocks = same_columns(recomputed[at][...], jnp.concatenate(columns, axis=1))
                pair[0], pair[1] = jnp.split(blocks, 2, axis=1)

        mine[at] = pair[0]
        swap[at] = pair[1].astype(BF16)
        mirrors[at][here, :] = pair[0].T.astype(BF16)
        mirrors[at][there, :] = pair[1].T.astype(BF16)


def own_kernel(own_send, own_keep, other_send, other_keep, out):
    cells = own_send.shape[0]
    sides = ((own_send[...], other_send[...]), (own_keep[...], other_keep[...]))
    _, _, core = position()
    both = functools.reduce(jnp.add, [same_columns(own, jnp.concatenate([own, other], axis=0)) for own, other in sides])
    out[rows_of(core, cells), :] = both[:, :cells]
    out[rows_of(1 - core, cells), :] = both[:, cells:].T


def late_kernel(odds, own_keep, other_keep, *refs):
    count, (_, _, core) = len(odds), position()
    received, mine, swap, mirrors = refs[:count], refs[count], refs[count + 1], refs[count + 2 :]
    cells = own_keep.shape[0]
    here, there = rows_of(core, cells), rows_of(1 - core, cells)
    rows = jnp.concatenate([r[...] for r in received], axis=0)
    blocks = same_columns(rows, jnp.concatenate([own_keep[...], other_keep[...]], axis=0))
    for at in range(count):
        block, across = jnp.split(blocks[at * cells : (at + 1) * cells], 2, axis=1)
        mine[at] = block
        swap[at] = across.astype(BF16)
        mirrors[at][here, :] = block.astype(BF16).T
        mirrors[at][there, :] = across.astype(BF16).T


def diagonal(cells):
    return lax.broadcasted_iota(I32, (cells, cells), 0) == lax.broadcasted_iota(I32, (cells, cells), 1)


def combine_kernel(evens, odds, own_block, *refs):
    (mine_group, chip, core), every = position(), refs[-1]
    cells = own_block.shape[1]
    here, there = rows_of(core, cells), rows_of(1 - core, cells)
    every[0] = own_block[...]
    at = 0
    for group in (evens, odds):
        mine, swapped, mirrored = refs[at], refs[at + 1], refs[at + 2 : at + 2 + len(group)]
        at += 2 + len(group)
        for i, d in enumerate(group):
            every[d, here, :] = mine[i] + mirrored[i][here, :].astype(F32)
            every[d, there, :] = swapped[i].astype(F32) + mirrored[i][there, :].astype(F32)
    out_own, outs = refs[at], refs[at + 1 : -1]
    first = jnp.bitwise_xor(mine_group, chip)
    out_own[...] = every[first]
    for k, out in enumerate(outs, 1):
        d = jnp.bitwise_xor(first, k)
        out[: 2 * cells, :] = every[d].astype(BF16)
        square = every[d, here, :]
        lost = jnp.where(diagonal(cells), square - square.astype(BF16).astype(F32), 0.0)
        out[2 * cells :, :] = jnp.broadcast_to(jnp.sum(lost, axis=0, keepdims=True), (16, cells)).astype(BF16)


def final_kernel(amount, own, *refs):
    received, out = refs[:-1], refs[-1]
    cells = own.shape[1]
    total = own[...]
    for part in received:
        total = total + part[: 2 * cells, :].astype(F32)
    out[...] = total / amount
    lost = functools.reduce(jnp.add, [part[2 * cells : 2 * cells + 1, :].astype(F32) for part in received])
    here = rows_of(position()[2], cells)
    out[here, :] += jnp.where(diagonal(cells), lost / amount, 0.0)


def whole_call(kernel, name, shapes, scratch, *arrays, flops=1000):
    vmem = pl.BlockSpec(memory_space=pltpu.VMEM)
    many = isinstance(shapes, list)
    return pl.pallas_call(
        kernel,
        in_specs=[vmem] * len(arrays),
        out_specs=[vmem] * len(shapes) if many else vmem,
        out_shape=shapes,
        scratch_shapes=scratch,
        compiler_params=params(),
        cost_estimate=pl.CostEstimate(flops=flops, bytes_accessed=1, transcendentals=0),
        name=name,
    )(*arrays)


def per_device(grads, quads, volume, weight):
    groups, devices = lax.axis_size("elec"), lax.axis_size("cell")
    chips = devices // 2
    cells, measured = grads.shape[2], quads.shape[0]
    half, far = groups // 2, groups - 1
    odds = [d for d in range(1, chips) if odd(d)]
    evens = [d for d in range(1, chips) if not odd(d)]
    packed = pack(grads, volume)
    shape = grads.shape
    gradients = lambda x: x[: 3 * shape[1], :].reshape(shape)
    shards = {0: grads, far: hop(grads, "elec", groups, far)}
    for j in range(1, half):
        shards[j] = gradients(hop(packed, "elec", groups, j))
    for j in range(1, half):
        shards[far ^ j] = hop(shards[far], "elec", groups, j)

    bits = max(1, (chips - 1).bit_length())
    columns, weights = quads.T, weight.reshape(1, measured)
    volumes = volume.reshape(1, cells)
    relayed = {far ^ j: shards[far ^ j] for j in range(1, half)}
    direct = {k: shards[k] for k in shards if k not in relayed}
    ready = tuple(sorted(direct))
    turned = turn_shards([direct[k] for k in ready])

    across, volumes_across = {}, {}
    for d in evens:
        near = hop(packed, "cell", devices, 2 * d)
        near, volumes_across[d] = gradients(near), near[3 * shape[1] :, :]
        across[d] = {0: near}
        for k in [far, *range(1, half)]:
            across[d][k] = hop(shards[k], "cell", devices, 2 * d)

    form = functools.partial(sensitivities, bits=bits)
    own_send = form("send", quads=columns, weight=weights, volume=volumes, shards=relayed, turned=turned, ready=ready)
    received = [hop(own_send, "cell", devices, 2 * d) for d in odds]
    other_send = hop(own_send, "cell", devices, 1)
    columns, own_send, across = lax.optimization_barrier((columns, own_send, across))
    for d in evens:
        for j in range(1, half):
            across[d][far ^ j] = hop(across[d][far], "elec", groups, j)
    own_keep = form("keep", quads=columns, weight=weights, volume=volumes, shards=relayed, turned=turned, ready=ready)
    other_keep = hop(own_keep, "cell", devices, 1)
    recomputed = []
    for d in evens:
        recomputed.append(
            form(d, quads=columns, weight=weights, volume=volumes_across[d], shards=across[d], weigh=WEIGH)
        )

    whole, small = (2 * cells, cells), (cells, cells)
    outputs = lambda group: [
        jax.ShapeDtypeStruct((len(group), *small), F32),
        jax.ShapeDtypeStruct((len(group), *small), BF16),
    ] + [jax.ShapeDtypeStruct(whole, BF16)] * len(group)
    early = whole_call(
        functools.partial(early_kernel, evens),
        "early_blocks",
        outputs(evens),
        [pltpu.VMEM((2, *small), F32)],
        own_send, own_keep, other_send, other_keep, *recomputed,
    )
    late = whole_call(functools.partial(late_kernel, odds), "late_blocks", outputs(odds), [], own_keep, other_keep, *received)

    own_keep, late = lax.optimization_barrier((own_keep, late))
    own_block = whole_call(
        own_kernel, "own_block", jax.ShapeDtypeStruct(whole, F32), [], own_send, own_keep, other_send, other_keep
    )

    def exchange(group, mine, swap, *mirrors):
        moved = [hop(m, "cell", devices, 2 * d) for d, m in zip(group, mirrors)]
        return [mine, hop(swap, "cell", devices, 1)] + moved

    parts = whole_call(
        functools.partial(combine_kernel, evens, odds),
        "combine",
        [jax.ShapeDtypeStruct(whole, F32)] + [jax.ShapeDtypeStruct((2 * cells + 16, cells), BF16)] * (groups - 1),
        [pltpu.VMEM((chips, *whole), F32)],
        own_block, *exchange(evens, *early), *exchange(odds, *late),
    )
    arrived = [hop(parts[k], "elec", groups, k) for k in sorted(range(1, groups), key=lambda k: (k < half, k))]
    return whole_call(
        functools.partial(final_kernel, float(measured * groups)),
        "finish",
        jax.ShapeDtypeStruct(whole, F32),
        [],
        parts[0], *arrived,
    )


def solution(mesh):
    placed = (P(None, "elec", "cell"), P("elec", None), P("cell"), P("elec"))
    return jax.shard_map(
        per_device, mesh=mesh, in_specs=placed, out_specs=P("elec", "cell"), check_vma=False
    )
```

```python
import functools

import jax
import jax.numpy as jnp
from jax import lax
from jax.experimental import pallas as pl
from jax.experimental.pallas import tpu as pltpu
from jax.sharding import PartitionSpec as P

F32, BF16, I32 = jnp.float32, jnp.bfloat16, jnp.int32
WEIGH = 4
TILES = 4
LIMIT = 24 * 1024 * 1024


def params():
    return pltpu.CompilerParams(vmem_limit_bytes=LIMIT)


def hop(x, axis, size, mask):
    return lax.ppermute(x, axis, [(i, i ^ mask) for i in range(size)])


def odd(d):
    return bin(d).count("1") % 2 == 1


def position():
    here = lax.axis_index("cell")
    return lax.axis_index("elec"), jnp.right_shift(here, 1), jnp.bitwise_and(here, 1)


def bit_of(number, at):
    return jnp.bitwise_and(jnp.right_shift(number, at), 1)


def tiles_of(which, bits):
    _, chip, _ = position()
    keep = functools.reduce(jnp.bitwise_xor, [bit_of(chip, b) for b in range(bits)])
    send = 1 - keep
    if which == "send":
        return 2 * send, 2 * send + 1
    if which == "keep":
        return 2 * keep, 2 * keep + 1
    bit = bit_of(chip, low_bit(which))
    return 2 * send + bit, 2 * keep + bit


def low_bit(d):
    return (d & -d).bit_length() - 1


def difference_map(places, at, total):
    labels = lax.broadcasted_iota(jnp.int16, (total, places.shape[1]), 0)
    plus, minus = places[at : at + 1, :] == labels, places[at + 1 : at + 2, :] == labels
    one = jnp.ones((), BF16)
    return jnp.where(plus, one, jnp.where(minus, -one, jnp.zeros((), BF16)))


def turn(shards, turned, start=0):
    _, depth, cells = shards[0].shape
    for at, shard in enumerate(shards, start):
        for k in range(3):
            turned[k * cells : (k + 1) * cells, at * depth : (at + 1) * depth] = shard[k].T


def turn_kernel(*refs):
    turn(refs[:-1], refs[-1])


def turn_shards(shards):
    _, depth, cells = shards[0].shape
    return pl.pallas_call(
        turn_kernel,
        out_shape=jax.ShapeDtypeStruct((3 * cells, len(shards) * depth), BF16),
        compiler_params=params(),
        cost_estimate=pl.CostEstimate(flops=1000, bytes_accessed=1000, transcendentals=0),
        name="turn_shards",
    )(*shards)


def pack_kernel(shard, volume, quads, out, kept):
    parts, depth, cells = shard.shape
    kept[...] = quads[...]
    for k in range(parts):
        out[k * depth : (k + 1) * depth, :] = shard[k]
    rest = volume[...]
    rows = []
    for _ in range(3):
        rows.append(rest.astype(BF16).astype(F32))
        rest = rest - rows[-1]
    tail = jnp.concatenate(rows + [jnp.zeros((13, cells), F32)], axis=0)
    out[parts * depth :, :] = tail.astype(BF16)


def pack(shard, volume, quads):
    parts, depth, cells = shard.shape
    return pl.pallas_call(
        pack_kernel,
        out_shape=[jax.ShapeDtypeStruct((parts * depth + 16, cells), BF16), jax.ShapeDtypeStruct(quads.shape, I32)],
        compiler_params=params(),
        cost_estimate=pl.CostEstimate(flops=1000, bytes_accessed=1000, transcendentals=0),
        name="pack",
    )(shard, volume.reshape(1, cells), quads)


def products(offsets, rows, turned, depth):
    group, _, _ = position()
    total = len(offsets) * depth
    owner = rows // depth
    slot = jnp.bitwise_xor(owner, group)
    if offsets != tuple(range(len(offsets))):
        slot = functools.reduce(jnp.add, [jnp.where(slot == k, n + 1, 0) for n, k in enumerate(offsets)]) - 1
    places = (slot * depth + (rows - owner * depth)).astype(jnp.int16)
    return [
        jnp.dot(turned[:, :total], difference_map(places, at, total), preferred_element_type=F32) for at in (0, 2)
    ]


def tile_lanes(quads, tile):
    width = quads.shape[1] // TILES
    return pl.ds(pl.multiple_of(tile * width, width), width)


def partial_kernel(offsets, which, bits, quads, turned, out):
    width = quads.shape[1] // TILES
    for at, tile in enumerate(tiles_of(which, bits)):
        source, receiver = products(offsets, quads[:, tile_lanes(quads, tile)], turned, turned.shape[1] // len(offsets))
        out[0, :, at * width : (at + 1) * width] = source
        out[1, :, at * width : (at + 1) * width] = receiver


def sensitivity_kernel(offsets, ready, begun, which, bits, quads, weight, volume, *refs):
    shards, out, turned = refs[1 if ready or begun else 0 : -2], refs[-2], refs[-1]
    cells, width = out.shape[0], quads.shape[1] // TILES
    depth = turned.shape[1] // len(offsets)
    if ready:
        turned[:, : ready * depth] = refs[0][...]
    turn(shards, turned, ready)
    terms = volume[...].astype(F32)
    column = jnp.sum(jnp.broadcast_to(terms[:, None, :], (terms.shape[0], 8, cells)), axis=0).T[:, :1]
    for at, tile in enumerate(tiles_of(which, bits)):
        lanes = tile_lanes(quads, tile)
        source, receiver = products(offsets, quads[:, lanes], turned, depth)
        if begun:
            own = slice(at * width, (at + 1) * width)
            source, receiver = refs[0][0, :, own] + source, refs[0][1, :, own] + receiver
        product = source * receiver
        dots = product[:cells] + product[cells : 2 * cells] + product[2 * cells :]
        out[:, at * width : (at + 1) * width] = (weight[:, lanes] * -(column * dots)).astype(BF16)


def sensitivities(which, bits, quads, weight, volume, shards, turned=None, ready=(), begun=None, weigh=1):
    offsets = tuple(ready) + tuple(sorted(shards))
    held = [shards[k] for k in offsets[len(ready) :]]
    _, depth, cells = held[0].shape
    count, width = 2, quads.shape[1] // TILES
    first = [] if begun is None else [pltpu.with_memory_space_constraint(begun, pltpu.VMEM)]
    flops = weigh * 4 * count * width * len(offsets) * depth * 3 * cells
    return whole_call(
        functools.partial(sensitivity_kernel, offsets, len(ready), begun is not None, which, bits),
        "sensitivities",
        jax.ShapeDtypeStruct((cells, count * width), BF16),
        [pltpu.VMEM((3 * cells, len(offsets) * depth), BF16)],
        quads, weight, volume, *([turned] if ready else []), *first, *held,
        flops=flops,
    )


def partial_products(which, bits, quads, turned, offsets):
    rows, total = turned.shape
    count = quads.shape[1] * 2 // TILES
    return whole_call(
        functools.partial(partial_kernel, offsets, which, bits),
        "partial_products",
        pltpu.VMEM((2, rows, count), F32),
        [],
        quads, turned,
        flops=1000,
    )


def same_columns(left, right):
    return lax.dot_general(left, right, (((1,), (1,)), ((), ())), preferred_element_type=F32)


def rows_of(core, cells):
    return pl.ds(pl.multiple_of(core * cells, cells), cells)


def early_kernel(evens, own_send, own_keep, other_send, other_keep, *refs):
    count, (_, chip, core) = len(evens), position()
    recomputed, mine, swap = refs[:count], *refs[count : count + 2]
    mirrors, pair = refs[count + 2 : -1], refs[-1]
    cells = own_send.shape[0]
    here, there = rows_of(core, cells), rows_of(1 - core, cells)
    sides = ((0, own_send, other_send), (1, own_keep, other_keep))
    for at, d in enumerate(evens):
        part = own_send.shape[1] // 2
        for bit in range(2):

            @pl.when(bit_of(chip, low_bit(d)) == bit)
            def _():
                lanes = slice(bit * part, (bit + 1) * part)
                columns = [jnp.concatenate([own[:, lanes], other[:, lanes]], axis=0) for _, own, other in sides]
                blocks = same_columns(recomputed[at][...], jnp.concatenate(columns, axis=1))
                pair[0], pair[1] = jnp.split(blocks, 2, axis=1)

        mine[at] = pair[0]
        swap[at] = pair[1].astype(BF16)
        mirrors[at][here, :] = pair[0].T.astype(BF16)
        mirrors[at][there, :] = pair[1].T.astype(BF16)


def own_kernel(own_send, own_keep, other_send, other_keep, out):
    cells = own_send.shape[0]
    sides = ((own_send[...], other_send[...]), (own_keep[...], other_keep[...]))
    _, _, core = position()
    both = functools.reduce(jnp.add, [same_columns(own, jnp.concatenate([own, other], axis=0)) for own, other in sides])
    out[rows_of(core, cells), :] = both[:, :cells]
    out[rows_of(1 - core, cells), :] = both[:, cells:].T


def late_kernel(odds, own_keep, other_keep, *refs):
    count, (_, _, core) = len(odds), position()
    received, mine, swap, mirrors = refs[:count], refs[count], refs[count + 1], refs[count + 2 :]
    cells = own_keep.shape[0]
    here, there = rows_of(core, cells), rows_of(1 - core, cells)
    rows = jnp.concatenate([r[...] for r in received], axis=0)
    blocks = same_columns(rows, jnp.concatenate([own_keep[...], other_keep[...]], axis=0))
    for at in range(count):
        block, across = jnp.split(blocks[at * cells : (at + 1) * cells], 2, axis=1)
        mine[at] = block
        swap[at] = across.astype(BF16)
        mirrors[at][here, :] = block.astype(BF16).T
        mirrors[at][there, :] = across.astype(BF16).T


def diagonal(cells):
    return lax.broadcasted_iota(I32, (cells, cells), 0) == lax.broadcasted_iota(I32, (cells, cells), 1)


def combine_kernel(evens, odds, own_block, *refs):
    (mine_group, chip, core), every = position(), refs[-1]
    cells = own_block.shape[1]
    here, there = rows_of(core, cells), rows_of(1 - core, cells)
    every[0] = own_block[...]
    at = 0
    for group in (evens, odds):
        mine, swapped, mirrored = refs[at], refs[at + 1], refs[at + 2 : at + 2 + len(group)]
        at += 2 + len(group)
        for i, d in enumerate(group):
            every[d, here, :] = mine[i] + mirrored[i][here, :].astype(F32)
            every[d, there, :] = swapped[i].astype(F32) + mirrored[i][there, :].astype(F32)
    out_own, outs = refs[at], refs[at + 1 : -1]
    first = jnp.bitwise_xor(mine_group, chip)
    out_own[...] = every[first]
    for k, out in enumerate(outs, 1):
        d = jnp.bitwise_xor(first, k)
        out[: 2 * cells, :] = every[d].astype(BF16)
        square = every[d, here, :]
        lost = jnp.where(diagonal(cells), square - square.astype(BF16).astype(F32), 0.0)
        out[2 * cells :, :] = jnp.broadcast_to(jnp.sum(lost, axis=0, keepdims=True), (16, cells)).astype(BF16)


def final_kernel(amount, own, *refs):
    received, out = refs[:-1], refs[-1]
    cells = own.shape[1]
    total = own[...]
    for part in received:
        total = total + part[: 2 * cells, :].astype(F32)
    out[...] = total / amount
    lost = functools.reduce(jnp.add, [part[2 * cells : 2 * cells + 1, :].astype(F32) for part in received])
    here = rows_of(position()[2], cells)
    out[here, :] += jnp.where(diagonal(cells), lost / amount, 0.0)


def whole_call(kernel, name, shapes, scratch, *arrays, flops=1000):
    vmem = pl.BlockSpec(memory_space=pltpu.VMEM)
    many = isinstance(shapes, list)
    return pl.pallas_call(
        kernel,
        in_specs=[vmem] * len(arrays),
        out_specs=[vmem] * len(shapes) if many else vmem,
        out_shape=shapes,
        scratch_shapes=scratch,
        compiler_params=params(),
        cost_estimate=pl.CostEstimate(flops=flops, bytes_accessed=1, transcendentals=0),
        name=name,
    )(*arrays)


def per_device(grads, quads, volume, weight):
    groups, devices = lax.axis_size("elec"), lax.axis_size("cell")
    chips = devices // 2
    cells, measured = grads.shape[2], quads.shape[0]
    half, far = groups // 2, groups - 1
    odds = [d for d in range(1, chips) if odd(d)]
    evens = [d for d in range(1, chips) if not odd(d)]
    packed, columns = pack(grads, volume, quads.T)
    shape = grads.shape
    gradients = lambda x: x[: 3 * shape[1], :].reshape(shape)
    shards = {0: gradients(packed), far: hop(grads, "elec", groups, far)}
    for j in range(1, half):
        shards[j] = hop(grads, "elec", groups, j)
    for j in range(1, half):
        shards[far ^ j] = hop(shards[far], "elec", groups, j)

    bits = max(1, (chips - 1).bit_length())
    weights = weight.reshape(1, measured)
    volumes = volume.reshape(1, cells)
    relayed = {far ^ j: shards[far ^ j] for j in range(1, half)}
    direct = {k: shards[k] for k in shards if k not in relayed}
    ready = tuple(sorted(direct))
    turned = turn_shards([direct[k] for k in ready])

    across, volumes_across = {}, {}
    for d in evens:
        near = hop(packed, "cell", devices, 2 * d)
        near, volumes_across[d] = gradients(near), near[3 * shape[1] :, :]
        across[d] = {0: near}
        for k in [far, *range(1, half)]:
            across[d][k] = hop(shards[k], "cell", devices, 2 * d)

    form = functools.partial(sensitivities, bits=bits)
    begun = partial_products("send", bits, columns, turned, ready)
    own_send = form("send", quads=columns, weight=weights, volume=volumes, shards=relayed, begun=begun)
    received = [hop(own_send, "cell", devices, 2 * d) for d in odds]
    other_send = hop(own_send, "cell", devices, 1)
    columns, own_send, across = lax.optimization_barrier((columns, own_send, across))
    for d in evens:
        for j in range(1, half):
            across[d][far ^ j] = hop(across[d][far], "elec", groups, j)
    own_keep = form("keep", quads=columns, weight=weights, volume=volumes, shards=relayed, turned=turned, ready=ready)
    other_keep = hop(own_keep, "cell", devices, 1)
    recomputed = []
    for d in evens:
        recomputed.append(
            form(d, quads=columns, weight=weights, volume=volumes_across[d], shards=across[d], weigh=WEIGH)
        )

    whole, small = (2 * cells, cells), (cells, cells)
    outputs = lambda group: [
        jax.ShapeDtypeStruct((len(group), *small), F32),
        jax.ShapeDtypeStruct((len(group), *small), BF16),
    ] + [jax.ShapeDtypeStruct(whole, BF16)] * len(group)
    early = whole_call(
        functools.partial(early_kernel, evens),
        "early_blocks",
        outputs(evens),
        [pltpu.VMEM((2, *small), F32)],
        own_send, own_keep, other_send, other_keep, *recomputed,
    )
    late = whole_call(functools.partial(late_kernel, odds), "late_blocks", outputs(odds), [], own_keep, other_keep, *received)

    own_keep, late = lax.optimization_barrier((own_keep, late))
    own_block = whole_call(
        own_kernel, "own_block", jax.ShapeDtypeStruct(whole, F32), [], own_send, own_keep, other_send, other_keep
    )

    def exchange(group, mine, swap, *mirrors):
        moved = [hop(m, "cell", devices, 2 * d) for d, m in zip(group, mirrors)]
        return [mine, hop(swap, "cell", devices, 1)] + moved

    parts = whole_call(
        functools.partial(combine_kernel, evens, odds),
        "combine",
        [jax.ShapeDtypeStruct(whole, F32)] + [jax.ShapeDtypeStruct((2 * cells + 16, cells), BF16)] * (groups - 1),
        [pltpu.VMEM((chips, *whole), F32)],
        own_block, *exchange(evens, *early), *exchange(odds, *late),
    )
    arrived = [hop(parts[k], "elec", groups, k) for k in sorted(range(1, groups), key=lambda k: (k < half, k))]
    return whole_call(
        functools.partial(final_kernel, float(measured * groups)),
        "finish",
        jax.ShapeDtypeStruct(whole, F32),
        [],
        parts[0], *arrived,
    )


def solution(mesh):
    placed = (P(None, "elec", "cell"), P("elec", None), P("cell"), P("elec"))
    return jax.shard_map(
        per_device, mesh=mesh, in_specs=placed, out_specs=P("elec", "cell"), check_vma=False
    )
```

```python
import functools

import jax
import jax.numpy as jnp
from jax import lax
from jax.experimental import pallas as pl
from jax.experimental.pallas import tpu as pltpu
from jax.sharding import PartitionSpec as P

F32, BF16, I32 = jnp.float32, jnp.bfloat16, jnp.int32
WEIGH = 4
TILES = 4
LIMIT = 24 * 1024 * 1024


def params():
    return pltpu.CompilerParams(vmem_limit_bytes=LIMIT)


def hop(x, axis, size, mask):
    return lax.ppermute(x, axis, [(i, i ^ mask) for i in range(size)])


def odd(d):
    return bin(d).count("1") % 2 == 1


def position():
    here = lax.axis_index("cell")
    return lax.axis_index("elec"), jnp.right_shift(here, 1), jnp.bitwise_and(here, 1)


def bit_of(number, at):
    return jnp.bitwise_and(jnp.right_shift(number, at), 1)


def tiles_of(which, bits):
    _, chip, _ = position()
    keep = functools.reduce(jnp.bitwise_xor, [bit_of(chip, b) for b in range(bits)])
    send = 1 - keep
    if which == "send":
        return 2 * send, 2 * send + 1
    if which == "keep":
        return 2 * keep, 2 * keep + 1
    bit = bit_of(chip, low_bit(which))
    return 2 * send + bit, 2 * keep + bit


def low_bit(d):
    return (d & -d).bit_length() - 1


def difference_map(places, at, total):
    labels = lax.broadcasted_iota(jnp.int16, (total, places.shape[1]), 0)
    plus, minus = places[at : at + 1, :] == labels, places[at + 1 : at + 2, :] == labels
    one = jnp.ones((), BF16)
    return jnp.where(plus, one, jnp.where(minus, -one, jnp.zeros((), BF16)))


def turn(shards, turned, start=0):
    _, depth, cells = shards[0].shape
    for at, shard in enumerate(shards, start):
        for k in range(3):
            turned[k * cells : (k + 1) * cells, at * depth : (at + 1) * depth] = shard[k].T


def turn_kernel(*refs):
    turn(refs[:-1], refs[-1])


def turn_shards(shards):
    _, depth, cells = shards[0].shape
    return pl.pallas_call(
        turn_kernel,
        out_shape=jax.ShapeDtypeStruct((3 * cells, len(shards) * depth), BF16),
        compiler_params=params(),
        cost_estimate=pl.CostEstimate(flops=1000, bytes_accessed=1000, transcendentals=0),
        name="turn_shards",
    )(*shards)


def pack_kernel(shard, volume, quads, out, kept, rest, sems):
    parts, depth, cells = shard.shape
    pairs = [(shard.at[k], out.at[pl.ds(k * depth, depth)]) for k in range(parts)] + [(volume, rest), (quads, kept)]
    copies = [pltpu.make_async_copy(source, target, sems.at[n]) for n, (source, target) in enumerate(pairs)]
    for copy in copies:
        copy.start()
    for copy in copies:
        copy.wait()
    value = rest[...]
    rows = []
    for _ in range(3):
        rows.append(value.astype(BF16).astype(F32))
        value = value - rows[-1]
    tail = jnp.concatenate(rows + [jnp.zeros((13, cells), F32)], axis=0)
    out[parts * depth :, :] = tail.astype(BF16)


def pack(shard, volume, quads):
    parts, depth, cells = shard.shape
    volume = volume.reshape(1, cells)
    return pl.pallas_call(
        pack_kernel,
        in_specs=[pl.BlockSpec(memory_space=pl.ANY)] * 3,
        out_specs=[pl.BlockSpec(memory_space=pltpu.VMEM)] * 2,
        out_shape=[jax.ShapeDtypeStruct((parts * depth + 16, cells), BF16), jax.ShapeDtypeStruct(quads.shape, I32)],
        scratch_shapes=[pltpu.VMEM(volume.shape, F32), pltpu.SemaphoreType.DMA((parts + 2,))],
        compiler_params=params(),
        cost_estimate=pl.CostEstimate(flops=1000, bytes_accessed=1000, transcendentals=0),
        name="pack",
    )(*[pltpu.with_memory_space_constraint(x, pltpu.HBM) for x in (shard, volume, quads)])


def products(offsets, rows, turned, depth):
    group, _, _ = position()
    total = len(offsets) * depth
    owner = rows // depth
    slot = jnp.bitwise_xor(owner, group)
    if offsets != tuple(range(len(offsets))):
        slot = functools.reduce(jnp.add, [jnp.where(slot == k, n + 1, 0) for n, k in enumerate(offsets)]) - 1
    places = (slot * depth + (rows - owner * depth)).astype(jnp.int16)
    return [
        jnp.dot(turned[:, :total], difference_map(places, at, total), preferred_element_type=F32) for at in (0, 2)
    ]


def tile_lanes(quads, tile):
    width = quads.shape[1] // TILES
    return pl.ds(pl.multiple_of(tile * width, width), width)


def partial_kernel(offsets, which, bits, quads, turned, out):
    width = quads.shape[1] // TILES
    for at, tile in enumerate(tiles_of(which, bits)):
        source, receiver = products(offsets, quads[:, tile_lanes(quads, tile)], turned, turned.shape[1] // len(offsets))
        out[0, :, at * width : (at + 1) * width] = source
        out[1, :, at * width : (at + 1) * width] = receiver


def sensitivity_kernel(offsets, ready, begun, which, bits, quads, weight, volume, *refs):
    shards, out, turned = refs[1 if ready or begun else 0 : -2], refs[-2], refs[-1]
    cells, width = out.shape[0], quads.shape[1] // TILES
    depth = turned.shape[1] // len(offsets)
    if ready:
        turned[:, : ready * depth] = refs[0][...]
    turn(shards, turned, ready)
    terms = volume[...].astype(F32)
    column = jnp.sum(jnp.broadcast_to(terms[:, None, :], (terms.shape[0], 8, cells)), axis=0).T[:, :1]
    for at, tile in enumerate(tiles_of(which, bits)):
        lanes = tile_lanes(quads, tile)
        source, receiver = products(offsets, quads[:, lanes], turned, depth)
        if begun:
            own = slice(at * width, (at + 1) * width)
            source, receiver = refs[0][0, :, own] + source, refs[0][1, :, own] + receiver
        product = source * receiver
        dots = product[:cells] + product[cells : 2 * cells] + product[2 * cells :]
        out[:, at * width : (at + 1) * width] = (weight[:, lanes] * -(column * dots)).astype(BF16)


def sensitivities(which, bits, quads, weight, volume, shards, turned=None, ready=(), begun=None, weigh=1):
    offsets = tuple(ready) + tuple(sorted(shards))
    held = [shards[k] for k in offsets[len(ready) :]]
    _, depth, cells = held[0].shape
    count, width = 2, quads.shape[1] // TILES
    first = [] if begun is None else [pltpu.with_memory_space_constraint(begun, pltpu.VMEM)]
    flops = weigh * 4 * count * width * len(offsets) * depth * 3 * cells
    return whole_call(
        functools.partial(sensitivity_kernel, offsets, len(ready), begun is not None, which, bits),
        "sensitivities",
        jax.ShapeDtypeStruct((cells, count * width), BF16),
        [pltpu.VMEM((3 * cells, len(offsets) * depth), BF16)],
        quads, weight, volume, *([turned] if ready else []), *first, *held,
        flops=flops,
    )


def partial_products(which, bits, quads, turned, offsets):
    rows, total = turned.shape
    count = quads.shape[1] * 2 // TILES
    return whole_call(
        functools.partial(partial_kernel, offsets, which, bits),
        "partial_products",
        pltpu.VMEM((2, rows, count), F32),
        [],
        quads, turned,
        flops=1000,
    )


def same_columns(left, right):
    return lax.dot_general(left, right, (((1,), (1,)), ((), ())), preferred_element_type=F32)


def rows_of(core, cells):
    return pl.ds(pl.multiple_of(core * cells, cells), cells)


def early_kernel(evens, own_send, own_keep, other_send, other_keep, *refs):
    count, (_, chip, core) = len(evens), position()
    recomputed, mine, swap = refs[:count], *refs[count : count + 2]
    mirrors, pair = refs[count + 2 : -1], refs[-1]
    cells = own_send.shape[0]
    here, there = rows_of(core, cells), rows_of(1 - core, cells)
    sides = ((0, own_send, other_send), (1, own_keep, other_keep))
    for at, d in enumerate(evens):
        part = own_send.shape[1] // 2
        for bit in range(2):

            @pl.when(bit_of(chip, low_bit(d)) == bit)
            def _():
                lanes = slice(bit * part, (bit + 1) * part)
                columns = [jnp.concatenate([own[:, lanes], other[:, lanes]], axis=0) for _, own, other in sides]
                blocks = same_columns(recomputed[at][...], jnp.concatenate(columns, axis=1))
                pair[0], pair[1] = jnp.split(blocks, 2, axis=1)

        mine[at] = pair[0]
        swap[at] = pair[1].astype(BF16)
        mirrors[at][here, :] = pair[0].T.astype(BF16)
        mirrors[at][there, :] = pair[1].T.astype(BF16)


def own_kernel(own_send, own_keep, other_send, other_keep, out):
    cells = own_send.shape[0]
    sides = ((own_send[...], other_send[...]), (own_keep[...], other_keep[...]))
    _, _, core = position()
    both = functools.reduce(jnp.add, [same_columns(own, jnp.concatenate([own, other], axis=0)) for own, other in sides])
    out[rows_of(core, cells), :] = both[:, :cells]
    out[rows_of(1 - core, cells), :] = both[:, cells:].T


def late_kernel(odds, own_keep, other_keep, *refs):
    count, (_, _, core) = len(odds), position()
    received, mine, swap, mirrors = refs[:count], refs[count], refs[count + 1], refs[count + 2 :]
    cells = own_keep.shape[0]
    here, there = rows_of(core, cells), rows_of(1 - core, cells)
    rows = jnp.concatenate([r[...] for r in received], axis=0)
    blocks = same_columns(rows, jnp.concatenate([own_keep[...], other_keep[...]], axis=0))
    for at in range(count):
        block, across = jnp.split(blocks[at * cells : (at + 1) * cells], 2, axis=1)
        mine[at] = block
        swap[at] = across.astype(BF16)
        mirrors[at][here, :] = block.astype(BF16).T
        mirrors[at][there, :] = across.astype(BF16).T


def diagonal(cells):
    return lax.broadcasted_iota(I32, (cells, cells), 0) == lax.broadcasted_iota(I32, (cells, cells), 1)


def combine_kernel(evens, odds, own_block, *refs):
    (mine_group, chip, core), every = position(), refs[-1]
    cells = own_block.shape[1]
    here, there = rows_of(core, cells), rows_of(1 - core, cells)
    every[0] = own_block[...]
    at = 0
    for group in (evens, odds):
        mine, swapped, mirrored = refs[at], refs[at + 1], refs[at + 2 : at + 2 + len(group)]
        at += 2 + len(group)
        for i, d in enumerate(group):
            every[d, here, :] = mine[i] + mirrored[i][here, :].astype(F32)
            every[d, there, :] = swapped[i].astype(F32) + mirrored[i][there, :].astype(F32)
    out_own, outs = refs[at], refs[at + 1 : -1]
    first = jnp.bitwise_xor(mine_group, chip)
    out_own[...] = every[first]
    for k, out in enumerate(outs, 1):
        d = jnp.bitwise_xor(first, k)
        out[: 2 * cells, :] = every[d].astype(BF16)
        square = every[d, here, :]
        lost = jnp.where(diagonal(cells), square - square.astype(BF16).astype(F32), 0.0)
        out[2 * cells :, :] = jnp.broadcast_to(jnp.sum(lost, axis=0, keepdims=True), (16, cells)).astype(BF16)


def final_kernel(amount, own, *refs):
    received, out = refs[:-1], refs[-1]
    cells = own.shape[1]
    total = own[...]
    for part in received:
        total = total + part[: 2 * cells, :].astype(F32)
    out[...] = total / amount
    lost = functools.reduce(jnp.add, [part[2 * cells :, :].astype(F32)[:1] for part in received])
    here = rows_of(position()[2], cells)
    out[here, :] += jnp.where(diagonal(cells), lost / amount, 0.0)


def whole_call(kernel, name, shapes, scratch, *arrays, flops=1000):
    vmem = pl.BlockSpec(memory_space=pltpu.VMEM)
    many = isinstance(shapes, list)
    return pl.pallas_call(
        kernel,
        in_specs=[vmem] * len(arrays),
        out_specs=[vmem] * len(shapes) if many else vmem,
        out_shape=shapes,
        scratch_shapes=scratch,
        compiler_params=params(),
        cost_estimate=pl.CostEstimate(flops=flops, bytes_accessed=1, transcendentals=0),
        name=name,
    )(*arrays)


def per_device(grads, quads, volume, weight):
    groups, devices = lax.axis_size("elec"), lax.axis_size("cell")
    chips = devices // 2
    cells, measured = grads.shape[2], quads.shape[0]
    half, far = groups // 2, groups - 1
    odds = [d for d in range(1, chips) if odd(d)]
    evens = [d for d in range(1, chips) if not odd(d)]
    packed, columns = pack(grads, volume, quads.T)
    shape = grads.shape
    gradients = lambda x: x[: 3 * shape[1], :].reshape(shape)
    shards = {0: gradients(packed), far: hop(grads, "elec", groups, far)}
    for j in range(1, half):
        shards[j] = hop(grads, "elec", groups, j)
    for j in range(1, half):
        shards[far ^ j] = hop(shards[far], "elec", groups, j)

    bits = max(1, (chips - 1).bit_length())
    weights = weight.reshape(1, measured)
    volumes = volume.reshape(1, cells)
    relayed = {far ^ j: shards[far ^ j] for j in range(1, half)}
    direct = {k: shards[k] for k in shards if k not in relayed}
    ready = tuple(sorted(direct))
    turned = turn_shards([direct[k] for k in ready])

    across, volumes_across = {}, {}
    for d in evens:
        near = hop(packed, "cell", devices, 2 * d)
        near, volumes_across[d] = gradients(near), near[3 * shape[1] :, :]
        across[d] = {0: near}
        for k in [far, *range(1, half)]:
            across[d][k] = hop(shards[k], "cell", devices, 2 * d)

    form = functools.partial(sensitivities, bits=bits)
    begun = partial_products("send", bits, columns, turned, ready)
    own_send = form("send", quads=columns, weight=weights, volume=volumes, shards=relayed, begun=begun)
    received = [hop(own_send, "cell", devices, 2 * d) for d in odds]
    other_send = hop(own_send, "cell", devices, 1)
    first = {d: {k: across[d][k] for k in (0, far)} for d in evens}
    columns, own_send, first = lax.optimization_barrier((columns, own_send, first))
    across = {d: {**across[d], **first[d]} for d in evens}
    for d in evens:
        for j in range(1, half):
            across[d][far ^ j] = hop(across[d][far], "elec", groups, j)
    own_keep = form("keep", quads=columns, weight=weights, volume=volumes, shards=relayed, turned=turned, ready=ready)
    other_keep = hop(own_keep, "cell", devices, 1)
    recomputed = []
    for d in evens:
        recomputed.append(
            form(d, quads=columns, weight=weights, volume=volumes_across[d], shards=across[d], weigh=WEIGH)
        )

    whole, small = (2 * cells, cells), (cells, cells)
    outputs = lambda group: [
        jax.ShapeDtypeStruct((len(group), *small), F32),
        jax.ShapeDtypeStruct((len(group), *small), BF16),
    ] + [jax.ShapeDtypeStruct(whole, BF16)] * len(group)
    early = whole_call(
        functools.partial(early_kernel, evens),
        "early_blocks",
        outputs(evens),
        [pltpu.VMEM((2, *small), F32)],
        own_send, own_keep, other_send, other_keep, *recomputed,
    )
    late = whole_call(functools.partial(late_kernel, odds), "late_blocks", outputs(odds), [], own_keep, other_keep, *received)

    own_keep, late = lax.optimization_barrier((own_keep, late))
    own_block = whole_call(
        own_kernel, "own_block", jax.ShapeDtypeStruct(whole, F32), [], own_send, own_keep, other_send, other_keep
    )

    def exchange(group, mine, swap, *mirrors):
        moved = [hop(m, "cell", devices, 2 * d) for d, m in zip(group, mirrors)]
        return [mine, hop(swap, "cell", devices, 1)] + moved

    parts = whole_call(
        functools.partial(combine_kernel, evens, odds),
        "combine",
        [jax.ShapeDtypeStruct(whole, F32)] + [jax.ShapeDtypeStruct((2 * cells + 16, cells), BF16)] * (groups - 1),
        [pltpu.VMEM((chips, *whole), F32)],
        own_block, *exchange(evens, *early), *exchange(odds, *late),
    )
    arrived = [hop(parts[k], "elec", groups, k) for k in sorted(range(1, groups), key=lambda k: (k < half, k))]
    return whole_call(
        functools.partial(final_kernel, float(measured * groups)),
        "finish",
        jax.ShapeDtypeStruct(whole, F32),
        [],
        parts[0], *arrived,
    )


def solution(mesh):
    placed = (P(None, "elec", "cell"), P("elec", None), P("cell"), P("elec"))
    return jax.shard_map(
        per_device, mesh=mesh, in_specs=placed, out_specs=P("elec", "cell"), check_vma=False
    )
```

```python
import functools

import jax
import jax.numpy as jnp
from jax import lax
from jax.experimental import pallas as pl
from jax.experimental.pallas import tpu as pltpu
from jax.sharding import PartitionSpec as P

F32, BF16, I32 = jnp.float32, jnp.bfloat16, jnp.int32
WEIGH = 16
TILES = 4
LIMIT = 24 * 1024 * 1024


def params():
    return pltpu.CompilerParams(vmem_limit_bytes=LIMIT)


def hop(x, axis, size, mask):
    return lax.ppermute(x, axis, [(i, i ^ mask) for i in range(size)])


def odd(d):
    return bin(d).count("1") % 2 == 1


def position():
    here = lax.axis_index("cell")
    return lax.axis_index("elec"), jnp.right_shift(here, 1), jnp.bitwise_and(here, 1)


def bit_of(number, at):
    return jnp.bitwise_and(jnp.right_shift(number, at), 1)


def tiles_of(which, bits):
    _, chip, _ = position()
    keep = functools.reduce(jnp.bitwise_xor, [bit_of(chip, b) for b in range(bits)])
    send = 1 - keep
    if which == "send":
        return 2 * send, 2 * send + 1
    if which == "keep":
        return 2 * keep, 2 * keep + 1
    bit = bit_of(chip, low_bit(which))
    return 2 * send + bit, 2 * keep + bit


def low_bit(d):
    return (d & -d).bit_length() - 1


def difference_map(places, at, total):
    labels = lax.broadcasted_iota(jnp.int16, (total, places.shape[1]), 0)
    plus, minus = places[at : at + 1, :] == labels, places[at + 1 : at + 2, :] == labels
    one = jnp.ones((), BF16)
    return jnp.where(plus, one, jnp.where(minus, -one, jnp.zeros((), BF16)))


def turn(shards, turned, start=0):
    _, depth, cells = shards[0].shape
    for at, shard in enumerate(shards, start):
        for k in range(3):
            turned[k * cells : (k + 1) * cells, at * depth : (at + 1) * depth] = shard[k].T


def turn_kernel(*refs):
    turn(refs[:-1], refs[-1])


def turn_shards(shards):
    _, depth, cells = shards[0].shape
    return pl.pallas_call(
        turn_kernel,
        out_shape=jax.ShapeDtypeStruct((3 * cells, len(shards) * depth), BF16),
        compiler_params=params(),
        cost_estimate=pl.CostEstimate(flops=1000, bytes_accessed=1000, transcendentals=0),
        name="turn_shards",
    )(*shards)


def pack_kernel(shard, volume, quads, out, kept, rest, sems):
    parts, depth, cells = shard.shape
    pairs = [(shard.at[k], out.at[pl.ds(k * depth, depth)]) for k in range(parts)] + [(volume, rest), (quads, kept)]
    copies = [pltpu.make_async_copy(source, target, sems.at[n]) for n, (source, target) in enumerate(pairs)]
    for copy in copies:
        copy.start()
    for copy in copies:
        copy.wait()
    value = rest[...]
    rows = []
    for _ in range(3):
        rows.append(value.astype(BF16).astype(F32))
        value = value - rows[-1]
    tail = jnp.concatenate(rows + [jnp.zeros((13, cells), F32)], axis=0)
    out[parts * depth :, :] = tail.astype(BF16)


def pack(shard, volume, quads):
    parts, depth, cells = shard.shape
    volume = volume.reshape(1, cells)
    return pl.pallas_call(
        pack_kernel,
        in_specs=[pl.BlockSpec(memory_space=pl.ANY)] * 3,
        out_specs=[pl.BlockSpec(memory_space=pltpu.VMEM)] * 2,
        out_shape=[jax.ShapeDtypeStruct((parts * depth + 16, cells), BF16), jax.ShapeDtypeStruct(quads.shape, I32)],
        scratch_shapes=[pltpu.VMEM(volume.shape, F32), pltpu.SemaphoreType.DMA((parts + 2,))],
        compiler_params=params(),
        cost_estimate=pl.CostEstimate(flops=1000, bytes_accessed=1000, transcendentals=0),
        name="pack",
    )(*[pltpu.with_memory_space_constraint(x, pltpu.HBM) for x in (shard, volume, quads)])


def products(offsets, rows, turned, depth):
    group, _, _ = position()
    total = len(offsets) * depth
    owner = rows // depth
    slot = jnp.bitwise_xor(owner, group)
    if offsets != tuple(range(len(offsets))):
        slot = functools.reduce(jnp.add, [jnp.where(slot == k, n + 1, 0) for n, k in enumerate(offsets)]) - 1
    places = (slot * depth + (rows - owner * depth)).astype(jnp.int16)
    return [
        jnp.dot(turned[:, :total], difference_map(places, at, total), preferred_element_type=F32) for at in (0, 2)
    ]


def tile_lanes(quads, tile):
    width = quads.shape[1] // TILES
    return pl.ds(pl.multiple_of(tile * width, width), width)


def partial_kernel(offsets, which, bits, quads, turned, out):
    width = quads.shape[1] // TILES
    for at, tile in enumerate(tiles_of(which, bits)):
        source, receiver = products(offsets, quads[:, tile_lanes(quads, tile)], turned, turned.shape[1] // len(offsets))
        out[0, :, at * width : (at + 1) * width] = source
        out[1, :, at * width : (at + 1) * width] = receiver


def sensitivity_kernel(offsets, ready, begun, which, bits, quads, weight, volume, *refs):
    shards, out, turned = refs[1 if ready or begun else 0 : -2], refs[-2], refs[-1]
    cells, width = out.shape[0], quads.shape[1] // TILES
    depth = turned.shape[1] // len(offsets)
    if ready:
        turned[:, : ready * depth] = refs[0][...]
    turn(shards, turned, ready)
    terms = volume[...].astype(F32)
    column = jnp.sum(jnp.broadcast_to(terms[:, None, :], (terms.shape[0], 8, cells)), axis=0).T[:, :1]
    for at, tile in enumerate(tiles_of(which, bits)):
        lanes = tile_lanes(quads, tile)
        source, receiver = products(offsets, quads[:, lanes], turned, depth)
        if begun:
            own = slice(at * width, (at + 1) * width)
            source, receiver = refs[0][0, :, own] + source, refs[0][1, :, own] + receiver
        product = source * receiver
        dots = product[:cells] + product[cells : 2 * cells] + product[2 * cells :]
        out[:, at * width : (at + 1) * width] = (weight[:, lanes] * -(column * dots)).astype(BF16)


def sensitivities(which, bits, quads, weight, volume, shards, turned=None, ready=(), begun=None, weigh=1):
    offsets = tuple(ready) + tuple(sorted(shards))
    held = [shards[k] for k in offsets[len(ready) :]]
    _, depth, cells = held[0].shape
    count, width = 2, quads.shape[1] // TILES
    first = [] if begun is None else [pltpu.with_memory_space_constraint(begun, pltpu.VMEM)]
    flops = weigh * 4 * count * width * len(offsets) * depth * 3 * cells
    return whole_call(
        functools.partial(sensitivity_kernel, offsets, len(ready), begun is not None, which, bits),
        "sensitivities",
        jax.ShapeDtypeStruct((cells, count * width), BF16),
        [pltpu.VMEM((3 * cells, len(offsets) * depth), BF16)],
        quads, weight, volume, *([turned] if ready else []), *first, *held,
        flops=flops,
    )


def partial_products(which, bits, quads, turned, offsets):
    rows, total = turned.shape
    count = quads.shape[1] * 2 // TILES
    return whole_call(
        functools.partial(partial_kernel, offsets, which, bits),
        "partial_products",
        pltpu.VMEM((2, rows, count), F32),
        [],
        quads, turned,
        flops=1000,
    )


def same_columns(left, right):
    return lax.dot_general(left, right, (((1,), (1,)), ((), ())), preferred_element_type=F32)


def rows_of(core, cells):
    return pl.ds(pl.multiple_of(core * cells, cells), cells)


def early_kernel(evens, own_send, own_keep, other_send, other_keep, *refs):
    count, (_, chip, core) = len(evens), position()
    recomputed, mine, swap = refs[:count], *refs[count : count + 2]
    mirrors, pair = refs[count + 2 : -1], refs[-1]
    cells = own_send.shape[0]
    here, there = rows_of(core, cells), rows_of(1 - core, cells)
    sides = ((0, own_send, other_send), (1, own_keep, other_keep))
    for at, d in enumerate(evens):
        part = own_send.shape[1] // 2
        for bit in range(2):

            @pl.when(bit_of(chip, low_bit(d)) == bit)
            def _():
                lanes = slice(bit * part, (bit + 1) * part)
                columns = [jnp.concatenate([own[:, lanes], other[:, lanes]], axis=0) for _, own, other in sides]
                blocks = same_columns(recomputed[at][...], jnp.concatenate(columns, axis=1))
                pair[0], pair[1] = jnp.split(blocks, 2, axis=1)

        mine[at] = pair[0]
        swap[at] = pair[1].astype(BF16)
        mirrors[at][here, :] = pair[0].T.astype(BF16)
        mirrors[at][there, :] = pair[1].T.astype(BF16)


def own_kernel(own_send, own_keep, other_send, other_keep, out):
    cells = own_send.shape[0]
    sides = ((own_send[...], other_send[...]), (own_keep[...], other_keep[...]))
    _, _, core = position()
    both = functools.reduce(jnp.add, [same_columns(own, jnp.concatenate([own, other], axis=0)) for own, other in sides])
    out[rows_of(core, cells), :] = both[:, :cells]
    out[rows_of(1 - core, cells), :] = both[:, cells:].T


def late_kernel(odds, own_keep, other_keep, *refs):
    count, (_, _, core) = len(odds), position()
    received, mine, swap, mirrors = refs[:count], refs[count], refs[count + 1], refs[count + 2 :]
    cells = own_keep.shape[0]
    here, there = rows_of(core, cells), rows_of(1 - core, cells)
    rows = jnp.concatenate([r[...] for r in received], axis=0)
    blocks = same_columns(rows, jnp.concatenate([own_keep[...], other_keep[...]], axis=0))
    for at in range(count):
        block, across = jnp.split(blocks[at * cells : (at + 1) * cells], 2, axis=1)
        mine[at] = block
        swap[at] = across.astype(BF16)
        mirrors[at][here, :] = block.astype(BF16).T
        mirrors[at][there, :] = across.astype(BF16).T


def diagonal(cells):
    return lax.broadcasted_iota(I32, (cells, cells), 0) == lax.broadcasted_iota(I32, (cells, cells), 1)


def combine_kernel(evens, odds, own_block, *refs):
    (mine_group, chip, core), every = position(), refs[-1]
    cells = own_block.shape[1]
    here, there = rows_of(core, cells), rows_of(1 - core, cells)
    every[0] = own_block[...]
    at = 0
    for group in (evens, odds):
        mine, swapped, mirrored = refs[at], refs[at + 1], refs[at + 2 : at + 2 + len(group)]
        at += 2 + len(group)
        for i, d in enumerate(group):
            every[d, here, :] = mine[i] + mirrored[i][here, :].astype(F32)
            every[d, there, :] = swapped[i].astype(F32) + mirrored[i][there, :].astype(F32)
    out_own, outs = refs[at], refs[at + 1 : -1]
    first = jnp.bitwise_xor(mine_group, chip)
    out_own[...] = every[first]
    for k, out in enumerate(outs, 1):
        d = jnp.bitwise_xor(first, k)
        out[: 2 * cells, :] = every[d].astype(BF16)
        square = every[d, here, :]
        lost = jnp.where(diagonal(cells), square - square.astype(BF16).astype(F32), 0.0)
        out[2 * cells :, :] = jnp.broadcast_to(jnp.sum(lost, axis=0, keepdims=True), (16, cells)).astype(BF16)


def final_kernel(amount, own, *refs):
    received, out = refs[:-1], refs[-1]
    cells = own.shape[1]
    total = own[...]
    for part in received:
        total = total + part[: 2 * cells, :].astype(F32)
    out[...] = total / amount
    lost = functools.reduce(jnp.add, [part[2 * cells :, :].astype(F32)[:1] for part in received])
    here = rows_of(position()[2], cells)
    out[here, :] += jnp.where(diagonal(cells), lost / amount, 0.0)


def whole_call(kernel, name, shapes, scratch, *arrays, flops=1000):
    vmem = pl.BlockSpec(memory_space=pltpu.VMEM)
    many = isinstance(shapes, list)
    return pl.pallas_call(
        kernel,
        in_specs=[vmem] * len(arrays),
        out_specs=[vmem] * len(shapes) if many else vmem,
        out_shape=shapes,
        scratch_shapes=scratch,
        compiler_params=params(),
        cost_estimate=pl.CostEstimate(flops=flops, bytes_accessed=1, transcendentals=0),
        name=name,
    )(*arrays)


def per_device(grads, quads, volume, weight):
    groups, devices = lax.axis_size("elec"), lax.axis_size("cell")
    chips = devices // 2
    cells, measured = grads.shape[2], quads.shape[0]
    half, far = groups // 2, groups - 1
    odds = [d for d in range(1, chips) if odd(d)]
    evens = [d for d in range(1, chips) if not odd(d)]
    packed, columns = pack(grads, volume, quads.T)
    shape = grads.shape
    gradients = lambda x: x[: 3 * shape[1], :].reshape(shape)
    shards = {0: gradients(packed), far: hop(grads, "elec", groups, far)}
    for j in range(1, half):
        shards[j] = hop(grads, "elec", groups, j)
    for j in range(1, half):
        shards[far ^ j] = hop(shards[far], "elec", groups, j)

    bits = max(1, (chips - 1).bit_length())
    weights = weight.reshape(1, measured)
    volumes = volume.reshape(1, cells)
    relayed = {far ^ j: shards[far ^ j] for j in range(1, half)}
    direct = {k: shards[k] for k in shards if k not in relayed}
    ready = tuple(sorted(direct))
    turned = turn_shards([direct[k] for k in ready])

    across, volumes_across = {}, {}
    for d in evens:
        near = hop(packed, "cell", devices, 2 * d)
        near, volumes_across[d] = gradients(near), near[3 * shape[1] :, :]
        across[d] = {0: near}
        for k in [far, *range(1, half)]:
            across[d][k] = hop(shards[k], "cell", devices, 2 * d)

    form = functools.partial(sensitivities, bits=bits)
    begun = partial_products("send", bits, columns, turned, ready)
    own_send = form("send", quads=columns, weight=weights, volume=volumes, shards=relayed, begun=begun)
    received = [hop(own_send, "cell", devices, 2 * d) for d in odds]
    other_send = hop(own_send, "cell", devices, 1)
    first = {d: {k: across[d][k] for k in (0, far)} for d in evens}
    columns, own_send, first = lax.optimization_barrier((columns, own_send, first))
    across = {d: {**across[d], **first[d]} for d in evens}
    for d in evens:
        for j in range(1, half):
            across[d][far ^ j] = hop(across[d][far], "elec", groups, j)
    own_keep = form("keep", quads=columns, weight=weights, volume=volumes, shards=relayed, turned=turned, ready=ready)
    other_keep = hop(own_keep, "cell", devices, 1)
    recomputed = []
    for d in evens:
        turned = turn_shards([across[d][k] for k in ready])
        begun = partial_products(d, bits, columns, turned, ready)
        rest = {k: across[d][k] for k in across[d] if k not in ready}
        recomputed.append(
            form(d, quads=columns, weight=weights, volume=volumes_across[d], shards=rest, begun=begun, weigh=WEIGH)
        )

    whole, small = (2 * cells, cells), (cells, cells)
    outputs = lambda group: [
        jax.ShapeDtypeStruct((len(group), *small), F32),
        jax.ShapeDtypeStruct((len(group), *small), BF16),
    ] + [jax.ShapeDtypeStruct(whole, BF16)] * len(group)
    early = whole_call(
        functools.partial(early_kernel, evens),
        "early_blocks",
        outputs(evens),
        [pltpu.VMEM((2, *small), F32)],
        own_send, own_keep, other_send, other_keep, *recomputed,
    )
    late = whole_call(functools.partial(late_kernel, odds), "late_blocks", outputs(odds), [], own_keep, other_keep, *received)

    own_keep, late = lax.optimization_barrier((own_keep, late))
    own_block = whole_call(
        own_kernel, "own_block", jax.ShapeDtypeStruct(whole, F32), [], own_send, own_keep, other_send, other_keep
    )

    def exchange(group, mine, swap, *mirrors):
        moved = [hop(m, "cell", devices, 2 * d) for d, m in zip(group, mirrors)]
        return [mine, hop(swap, "cell", devices, 1)] + moved

    parts = whole_call(
        functools.partial(combine_kernel, evens, odds),
        "combine",
        [jax.ShapeDtypeStruct(whole, F32)] + [jax.ShapeDtypeStruct((2 * cells + 16, cells), BF16)] * (groups - 1),
        [pltpu.VMEM((chips, *whole), F32)],
        own_block, *exchange(evens, *early), *exchange(odds, *late),
    )
    arrived = [hop(parts[k], "elec", groups, k) for k in sorted(range(1, groups), key=lambda k: (k < half, k))]
    return whole_call(
        functools.partial(final_kernel, float(measured * groups)),
        "finish",
        jax.ShapeDtypeStruct(whole, F32),
        [],
        parts[0], *arrived,
    )


def solution(mesh):
    placed = (P(None, "elec", "cell"), P("elec", None), P("cell"), P("elec"))
    return jax.shard_map(
        per_device, mesh=mesh, in_specs=placed, out_specs=P("elec", "cell"), check_vma=False
    )
```

```python
import functools

import jax
import jax.numpy as jnp
from jax import lax
from jax.experimental import pallas as pl
from jax.experimental.pallas import tpu as pltpu
from jax.sharding import PartitionSpec as P

F32, BF16, I32 = jnp.float32, jnp.bfloat16, jnp.int32
WEIGH = 16
TILES = 4
LIMIT = 24 * 1024 * 1024


def params():
    return pltpu.CompilerParams(vmem_limit_bytes=LIMIT)


def hop(x, axis, size, mask):
    return lax.ppermute(x, axis, [(i, i ^ mask) for i in range(size)])


def odd(d):
    return bin(d).count("1") % 2 == 1


def position():
    here = lax.axis_index("cell")
    return lax.axis_index("elec"), jnp.right_shift(here, 1), jnp.bitwise_and(here, 1)


def bit_of(number, at):
    return jnp.bitwise_and(jnp.right_shift(number, at), 1)


def tiles_of(which, bits):
    _, chip, _ = position()
    keep = functools.reduce(jnp.bitwise_xor, [bit_of(chip, b) for b in range(bits)])
    send = 1 - keep
    if which == "send":
        return 2 * send, 2 * send + 1
    if which == "keep":
        return 2 * keep, 2 * keep + 1
    bit = bit_of(chip, low_bit(which))
    return 2 * send + bit, 2 * keep + bit


def low_bit(d):
    return (d & -d).bit_length() - 1


def difference_map(places, at, total):
    labels = lax.broadcasted_iota(jnp.int16, (total, places.shape[1]), 0)
    plus, minus = places[at : at + 1, :] == labels, places[at + 1 : at + 2, :] == labels
    one = jnp.ones((), BF16)
    return jnp.where(plus, one, jnp.where(minus, -one, jnp.zeros((), BF16)))


def turn(shards, turned, start=0):
    _, depth, cells = shards[0].shape
    for at, shard in enumerate(shards, start):
        for k in range(3):
            turned[k * cells : (k + 1) * cells, at * depth : (at + 1) * depth] = shard[k].T


def turn_kernel(*refs):
    turn(refs[:-1], refs[-1])


def turn_shards(shards):
    _, depth, cells = shards[0].shape
    return pl.pallas_call(
        turn_kernel,
        out_shape=jax.ShapeDtypeStruct((3 * cells, len(shards) * depth), BF16),
        compiler_params=params(),
        cost_estimate=pl.CostEstimate(flops=1000, bytes_accessed=1000, transcendentals=0),
        name="turn_shards",
    )(*shards)


def pack_kernel(shard, volume, quads, out, kept, rest, sems):
    parts, depth, cells = shard.shape
    pairs = [(shard.at[k], out.at[pl.ds(k * depth, depth)]) for k in range(parts)] + [(volume, rest), (quads, kept)]
    copies = [pltpu.make_async_copy(source, target, sems.at[n]) for n, (source, target) in enumerate(pairs)]
    for copy in copies:
        copy.start()
    for copy in copies:
        copy.wait()
    value = rest[...]
    rows = []
    for _ in range(3):
        rows.append(value.astype(BF16).astype(F32))
        value = value - rows[-1]
    tail = jnp.concatenate(rows + [jnp.zeros((13, cells), F32)], axis=0)
    out[parts * depth :, :] = tail.astype(BF16)


def pack(shard, volume, quads):
    parts, depth, cells = shard.shape
    volume = volume.reshape(1, cells)
    return pl.pallas_call(
        pack_kernel,
        in_specs=[pl.BlockSpec(memory_space=pl.ANY)] * 3,
        out_specs=[pl.BlockSpec(memory_space=pltpu.VMEM)] * 2,
        out_shape=[jax.ShapeDtypeStruct((parts * depth + 16, cells), BF16), jax.ShapeDtypeStruct(quads.shape, I32)],
        scratch_shapes=[pltpu.VMEM(volume.shape, F32), pltpu.SemaphoreType.DMA((parts + 2,))],
        compiler_params=params(),
        cost_estimate=pl.CostEstimate(flops=1000, bytes_accessed=1000, transcendentals=0),
        name="pack",
    )(*[pltpu.with_memory_space_constraint(x, pltpu.HBM) for x in (shard, volume, quads)])


def products(offsets, rows, turned, depth):
    group, _, _ = position()
    total = len(offsets) * depth
    owner = rows // depth
    slot = jnp.bitwise_xor(owner, group)
    if offsets != tuple(range(len(offsets))):
        slot = functools.reduce(jnp.add, [jnp.where(slot == k, n + 1, 0) for n, k in enumerate(offsets)]) - 1
    places = (slot * depth + (rows - owner * depth)).astype(jnp.int16)
    return [
        jnp.dot(turned[:, :total], difference_map(places, at, total), preferred_element_type=F32) for at in (0, 2)
    ]


def tile_lanes(quads, tile):
    width = quads.shape[1] // TILES
    return pl.ds(pl.multiple_of(tile * width, width), width)


def partial_kernel(offsets, which, bits, quads, turned, out):
    width = quads.shape[1] // TILES
    for at, tile in enumerate(tiles_of(which, bits)):
        source, receiver = products(offsets, quads[:, tile_lanes(quads, tile)], turned, turned.shape[1] // len(offsets))
        out[0, :, at * width : (at + 1) * width] = source
        out[1, :, at * width : (at + 1) * width] = receiver


def sensitivity_kernel(offsets, ready, begun, which, bits, quads, weight, volume, *refs):
    shards, out, turned = refs[1 if ready or begun else 0 : -2], refs[-2], refs[-1]
    cells, width = out.shape[0], quads.shape[1] // TILES
    depth = turned.shape[1] // len(offsets)
    if ready:
        turned[:, : ready * depth] = refs[0][...]
    turn(shards, turned, ready)
    terms = volume[...].astype(F32)
    column = jnp.sum(jnp.broadcast_to(terms[:, None, :], (terms.shape[0], 8, cells)), axis=0).T[:, :1]
    for at, tile in enumerate(tiles_of(which, bits)):
        lanes = tile_lanes(quads, tile)
        source, receiver = products(offsets, quads[:, lanes], turned, depth)
        if begun:
            own = slice(at * width, (at + 1) * width)
            source, receiver = refs[0][0, :, own] + source, refs[0][1, :, own] + receiver
        product = source * receiver
        dots = product[:cells] + product[cells : 2 * cells] + product[2 * cells :]
        out[:, at * width : (at + 1) * width] = (weight[:, lanes] * -(column * dots)).astype(BF16)


def sensitivities(which, bits, quads, weight, volume, shards, turned=None, ready=(), begun=None, weigh=1):
    offsets = tuple(ready) + tuple(sorted(shards))
    held = [shards[k] for k in offsets[len(ready) :]]
    _, depth, cells = held[0].shape
    count, width = 2, quads.shape[1] // TILES
    first = [] if begun is None else [pltpu.with_memory_space_constraint(begun, pltpu.VMEM)]
    flops = weigh * 4 * count * width * len(offsets) * depth * 3 * cells
    return whole_call(
        functools.partial(sensitivity_kernel, offsets, len(ready), begun is not None, which, bits),
        "sensitivities",
        jax.ShapeDtypeStruct((cells, count * width), BF16),
        [pltpu.VMEM((3 * cells, len(offsets) * depth), BF16)],
        quads, weight, volume, *([turned] if ready else []), *first, *held,
        flops=flops,
    )


def partial_products(which, bits, quads, turned, offsets):
    rows, total = turned.shape
    count = quads.shape[1] * 2 // TILES
    return whole_call(
        functools.partial(partial_kernel, offsets, which, bits),
        "partial_products",
        pltpu.VMEM((2, rows, count), F32),
        [],
        quads, turned,
        flops=1000,
    )


def same_columns(left, right):
    return lax.dot_general(left, right, (((1,), (1,)), ((), ())), preferred_element_type=F32)


def rows_of(core, cells):
    return pl.ds(pl.multiple_of(core * cells, cells), cells)


def early_kernel(evens, own_send, own_keep, other_send, other_keep, *refs):
    count, (_, chip, core) = len(evens), position()
    recomputed, mine, swap = refs[:count], *refs[count : count + 2]
    mirrors, pair = refs[count + 2 : -1], refs[-1]
    cells = own_send.shape[0]
    here, there = rows_of(core, cells), rows_of(1 - core, cells)
    sides = ((0, own_send, other_send), (1, own_keep, other_keep))
    for at, d in enumerate(evens):
        part = own_send.shape[1] // 2
        for bit in range(2):

            @pl.when(bit_of(chip, low_bit(d)) == bit)
            def _():
                lanes = slice(bit * part, (bit + 1) * part)
                columns = [jnp.concatenate([own[:, lanes], other[:, lanes]], axis=0) for _, own, other in sides]
                blocks = same_columns(recomputed[at][...], jnp.concatenate(columns, axis=1))
                pair[0], pair[1] = jnp.split(blocks, 2, axis=1)

        mine[at] = pair[0]
        swap[at] = pair[1].astype(BF16)
        mirrors[at][here, :] = pair[0].T.astype(BF16)
        mirrors[at][there, :] = pair[1].T.astype(BF16)


def own_kernel(own_send, own_keep, other_send, other_keep, out):
    cells = own_send.shape[0]
    sides = ((own_send[...], other_send[...]), (own_keep[...], other_keep[...]))
    _, _, core = position()
    both = functools.reduce(jnp.add, [same_columns(own, jnp.concatenate([own, other], axis=0)) for own, other in sides])
    out[rows_of(core, cells), :] = both[:, :cells]
    out[rows_of(1 - core, cells), :] = both[:, cells:].T


def late_kernel(odds, own_keep, other_keep, *refs):
    count, (_, _, core) = len(odds), position()
    received, mine, swap, mirrors = refs[:count], refs[count], refs[count + 1], refs[count + 2 :]
    cells = own_keep.shape[0]
    here, there = rows_of(core, cells), rows_of(1 - core, cells)
    rows = jnp.concatenate([r[...] for r in received], axis=0)
    blocks = same_columns(rows, jnp.concatenate([own_keep[...], other_keep[...]], axis=0))
    for at in range(count):
        block, across = jnp.split(blocks[at * cells : (at + 1) * cells], 2, axis=1)
        mine[at] = block
        swap[at] = across.astype(BF16)
        mirrors[at][here, :] = block.astype(BF16).T
        mirrors[at][there, :] = across.astype(BF16).T


def diagonal(cells):
    return lax.broadcasted_iota(I32, (cells, cells), 0) == lax.broadcasted_iota(I32, (cells, cells), 1)


def combine_kernel(evens, odds, own_block, *refs):
    (mine_group, chip, core), every = position(), refs[-1]
    cells = own_block.shape[1]
    here, there = rows_of(core, cells), rows_of(1 - core, cells)
    every[0] = own_block[...]
    at = 0
    for group in (evens, odds):
        mine, swapped, mirrored = refs[at], refs[at + 1], refs[at + 2 : at + 2 + len(group)]
        at += 2 + len(group)
        for i, d in enumerate(group):
            every[d, here, :] = mine[i] + mirrored[i][here, :].astype(F32)
            every[d, there, :] = swapped[i].astype(F32) + mirrored[i][there, :].astype(F32)
    out_own, outs = refs[at], refs[at + 1 : -1]
    first = jnp.bitwise_xor(mine_group, chip)
    out_own[...] = every[first]
    for k, out in enumerate(outs, 1):
        d = jnp.bitwise_xor(first, k)
        out[: 2 * cells, :] = every[d].astype(BF16)
        square = every[d, here, :]
        lost = jnp.where(diagonal(cells), square - square.astype(BF16).astype(F32), 0.0)
        out[2 * cells :, :] = jnp.broadcast_to(jnp.sum(lost, axis=0, keepdims=True), (16, cells)).astype(BF16)


def final_kernel(amount, own, *refs):
    received, out = refs[:-1], refs[-1]
    cells = own.shape[1]
    total = own[...]
    for part in received:
        total = total + part[: 2 * cells, :].astype(F32)
    out[...] = total / amount
    lost = functools.reduce(jnp.add, [part[2 * cells :, :].astype(F32)[:1] for part in received])
    here = rows_of(position()[2], cells)
    out[here, :] += jnp.where(diagonal(cells), lost / amount, 0.0)


def whole_call(kernel, name, shapes, scratch, *arrays, flops=1000):
    vmem = pl.BlockSpec(memory_space=pltpu.VMEM)
    many = isinstance(shapes, list)
    return pl.pallas_call(
        kernel,
        in_specs=[vmem] * len(arrays),
        out_specs=[vmem] * len(shapes) if many else vmem,
        out_shape=shapes,
        scratch_shapes=scratch,
        compiler_params=params(),
        cost_estimate=pl.CostEstimate(flops=flops, bytes_accessed=1, transcendentals=0),
        name=name,
    )(*arrays)


def per_device(grads, quads, volume, weight):
    groups, devices = lax.axis_size("elec"), lax.axis_size("cell")
    chips = devices // 2
    cells, measured = grads.shape[2], quads.shape[0]
    half, far = groups // 2, groups - 1
    odds = [d for d in range(1, chips) if odd(d)]
    evens = [d for d in range(1, chips) if not odd(d)]
    packed, columns = pack(grads, volume, quads.T)
    shape = grads.shape
    gradients = lambda x: x[: 3 * shape[1], :].reshape(shape)
    shards = {0: gradients(packed), far: hop(grads, "elec", groups, far)}
    for j in range(1, half):
        shards[j] = hop(grads, "elec", groups, j)
    for j in range(1, half):
        shards[far ^ j] = hop(shards[far], "elec", groups, j)

    bits = max(1, (chips - 1).bit_length())
    weights = weight.reshape(1, measured)
    volumes = volume.reshape(1, cells)
    relayed = {far ^ j: shards[far ^ j] for j in range(1, half)}
    relayed.update({j: shards[j] for j in range(1, half)})
    direct = {k: shards[k] for k in shards if k not in relayed}
    ready = tuple(sorted(direct))
    turned = turn_shards([direct[k] for k in ready])

    across, volumes_across = {}, {}
    for d in evens:
        near = hop(packed, "cell", devices, 2 * d)
        near, volumes_across[d] = gradients(near), near[3 * shape[1] :, :]
        across[d] = {0: near}
        for k in [far, *range(1, half)]:
            across[d][k] = hop(shards[k], "cell", devices, 2 * d)

    form = functools.partial(sensitivities, bits=bits)
    begun = partial_products("send", bits, columns, turned, ready)
    own_send = form("send", quads=columns, weight=weights, volume=volumes, shards=relayed, begun=begun)
    received = [hop(own_send, "cell", devices, 2 * d) for d in odds]
    other_send = hop(own_send, "cell", devices, 1)
    first = {d: {k: across[d][k] for k in (0, far)} for d in evens}
    columns, own_send, first = lax.optimization_barrier((columns, own_send, first))
    across = {d: {**across[d], **first[d]} for d in evens}
    for d in evens:
        for j in range(1, half):
            across[d][far ^ j] = hop(across[d][far], "elec", groups, j)
    own_keep = form("keep", quads=columns, weight=weights, volume=volumes, shards=relayed, turned=turned, ready=ready)
    other_keep = hop(own_keep, "cell", devices, 1)
    recomputed = []
    for d in evens:
        turned = turn_shards([across[d][k] for k in ready])
        begun = partial_products(d, bits, columns, turned, ready)
        rest = {k: across[d][k] for k in across[d] if k not in ready}
        recomputed.append(
            form(d, quads=columns, weight=weights, volume=volumes_across[d], shards=rest, begun=begun, weigh=WEIGH)
        )

    whole, small = (2 * cells, cells), (cells, cells)
    outputs = lambda group: [
        jax.ShapeDtypeStruct((len(group), *small), F32),
        jax.ShapeDtypeStruct((len(group), *small), BF16),
    ] + [jax.ShapeDtypeStruct(whole, BF16)] * len(group)
    early = whole_call(
        functools.partial(early_kernel, evens),
        "early_blocks",
        outputs(evens),
        [pltpu.VMEM((2, *small), F32)],
        own_send, own_keep, other_send, other_keep, *recomputed,
    )
    late = whole_call(functools.partial(late_kernel, odds), "late_blocks", outputs(odds), [], own_keep, other_keep, *received)

    own_keep, late = lax.optimization_barrier((own_keep, late))
    own_block = whole_call(
        own_kernel, "own_block", jax.ShapeDtypeStruct(whole, F32), [], own_send, own_keep, other_send, other_keep
    )

    def exchange(group, mine, swap, *mirrors):
        moved = [hop(m, "cell", devices, 2 * d) for d, m in zip(group, mirrors)]
        return [mine, hop(swap, "cell", devices, 1)] + moved

    parts = whole_call(
        functools.partial(combine_kernel, evens, odds),
        "combine",
        [jax.ShapeDtypeStruct(whole, F32)] + [jax.ShapeDtypeStruct((2 * cells + 16, cells), BF16)] * (groups - 1),
        [pltpu.VMEM((chips, *whole), F32)],
        own_block, *exchange(evens, *early), *exchange(odds, *late),
    )
    arrived = [hop(parts[k], "elec", groups, k) for k in sorted(range(1, groups), key=lambda k: (k < half, k))]
    return whole_call(
        functools.partial(final_kernel, float(measured * groups)),
        "finish",
        jax.ShapeDtypeStruct(whole, F32),
        [],
        parts[0], *arrived,
    )


def solution(mesh):
    placed = (P(None, "elec", "cell"), P("elec", None), P("cell"), P("elec"))
    return jax.shard_map(
        per_device, mesh=mesh, in_specs=placed, out_specs=P("elec", "cell"), check_vma=False
    )
```

```python
import functools

import jax
import jax.numpy as jnp
from jax import lax
from jax.experimental import pallas as pl
from jax.experimental.pallas import tpu as pltpu
from jax.sharding import PartitionSpec as P

F32, BF16, I32 = jnp.float32, jnp.bfloat16, jnp.int32
WEIGH = 16
TILES = 4
LIMIT = 24 * 1024 * 1024


def params():
    return pltpu.CompilerParams(vmem_limit_bytes=LIMIT)


def hop(x, axis, size, mask):
    return lax.ppermute(x, axis, [(i, i ^ mask) for i in range(size)])


def odd(d):
    return bin(d).count("1") % 2 == 1


def position():
    here = lax.axis_index("cell")
    return lax.axis_index("elec"), jnp.right_shift(here, 1), jnp.bitwise_and(here, 1)


def bit_of(number, at):
    return jnp.bitwise_and(jnp.right_shift(number, at), 1)


def tiles_of(which, bits):
    _, chip, _ = position()
    keep = functools.reduce(jnp.bitwise_xor, [bit_of(chip, b) for b in range(bits)])
    send = 1 - keep
    if which == "send":
        return 2 * send, 2 * send + 1
    if which == "keep":
        return 2 * keep, 2 * keep + 1
    bit = bit_of(chip, low_bit(which))
    return 2 * send + bit, 2 * keep + bit


def low_bit(d):
    return (d & -d).bit_length() - 1


def difference_map(places, at, total):
    labels = lax.broadcasted_iota(jnp.int16, (total, places.shape[1]), 0)
    plus, minus = places[at : at + 1, :] == labels, places[at + 1 : at + 2, :] == labels
    one = jnp.ones((), BF16)
    return jnp.where(plus, one, jnp.where(minus, -one, jnp.zeros((), BF16)))


def turn(shards, turned, start=0):
    _, depth, cells = shards[0].shape
    for at, shard in enumerate(shards, start):
        for k in range(3):
            turned[k * cells : (k + 1) * cells, at * depth : (at + 1) * depth] = shard[k].T


def turn_kernel(*refs):
    turn(refs[:-1], refs[-1])


def turn_shards(shards):
    _, depth, cells = shards[0].shape
    return pl.pallas_call(
        turn_kernel,
        out_shape=jax.ShapeDtypeStruct((3 * cells, len(shards) * depth), BF16),
        compiler_params=params(),
        cost_estimate=pl.CostEstimate(flops=1000, bytes_accessed=1000, transcendentals=0),
        name="turn_shards",
    )(*shards)


def pack_kernel(shard, volume, quads, out, kept, rest, sems):
    parts, depth, cells = shard.shape
    pairs = [(shard.at[k], out.at[pl.ds(k * depth, depth)]) for k in range(parts)] + [(volume, rest), (quads, kept)]
    copies = [pltpu.make_async_copy(source, target, sems.at[n]) for n, (source, target) in enumerate(pairs)]
    for copy in copies:
        copy.start()
    for copy in copies:
        copy.wait()
    value = rest[...]
    rows = []
    for _ in range(3):
        rows.append(value.astype(BF16).astype(F32))
        value = value - rows[-1]
    tail = jnp.concatenate(rows + [jnp.zeros((13, cells), F32)], axis=0)
    out[parts * depth :, :] = tail.astype(BF16)


def pack(shard, volume, quads):
    parts, depth, cells = shard.shape
    volume = volume.reshape(1, cells)
    return pl.pallas_call(
        pack_kernel,
        in_specs=[pl.BlockSpec(memory_space=pl.ANY)] * 3,
        out_specs=[pl.BlockSpec(memory_space=pltpu.VMEM)] * 2,
        out_shape=[jax.ShapeDtypeStruct((parts * depth + 16, cells), BF16), jax.ShapeDtypeStruct(quads.shape, I32)],
        scratch_shapes=[pltpu.VMEM(volume.shape, F32), pltpu.SemaphoreType.DMA((parts + 2,))],
        compiler_params=params(),
        cost_estimate=pl.CostEstimate(flops=1000, bytes_accessed=1000, transcendentals=0),
        name="pack",
    )(*[pltpu.with_memory_space_constraint(x, pltpu.HBM) for x in (shard, volume, quads)])


def products(offsets, rows, turned, depth):
    group, _, _ = position()
    total = len(offsets) * depth
    owner = rows // depth
    slot = jnp.bitwise_xor(owner, group)
    if offsets != tuple(range(len(offsets))):
        slot = functools.reduce(jnp.add, [jnp.where(slot == k, n + 1, 0) for n, k in enumerate(offsets)]) - 1
    places = (slot * depth + (rows - owner * depth)).astype(jnp.int16)
    return [
        jnp.dot(turned[:, :total], difference_map(places, at, total), preferred_element_type=F32) for at in (0, 2)
    ]


def tile_lanes(quads, tile):
    width = quads.shape[1] // TILES
    return pl.ds(pl.multiple_of(tile * width, width), width)


def partial_kernel(offsets, which, bits, quads, turned, out):
    width = quads.shape[1] // TILES
    for at, tile in enumerate(tiles_of(which, bits)):
        source, receiver = products(offsets, quads[:, tile_lanes(quads, tile)], turned, turned.shape[1] // len(offsets))
        out[0, :, at * width : (at + 1) * width] = source
        out[1, :, at * width : (at + 1) * width] = receiver


def sensitivity_kernel(offsets, ready, begun, which, bits, quads, weight, volume, *refs):
    shards, out, turned = refs[1 if ready or begun else 0 : -2], refs[-2], refs[-1]
    cells, width = out.shape[0], quads.shape[1] // TILES
    depth = turned.shape[1] // len(offsets)
    if ready:
        turned[:, : ready * depth] = refs[0][...]
    turn(shards, turned, ready)
    terms = volume[...].astype(F32)
    column = jnp.sum(jnp.broadcast_to(terms[:, None, :], (terms.shape[0], 8, cells)), axis=0).T[:, :1]
    for at, tile in enumerate(tiles_of(which, bits)):
        lanes = tile_lanes(quads, tile)
        source, receiver = products(offsets, quads[:, lanes], turned, depth)
        if begun:
            own = slice(at * width, (at + 1) * width)
            source, receiver = refs[0][0, :, own] + source, refs[0][1, :, own] + receiver
        product = source * receiver
        dots = product[:cells] + product[cells : 2 * cells] + product[2 * cells :]
        out[:, at * width : (at + 1) * width] = (weight[:, lanes] * -(column * dots)).astype(BF16)


def sensitivities(which, bits, quads, weight, volume, shards, turned=None, ready=(), begun=None, weigh=1):
    offsets = tuple(ready) + tuple(sorted(shards))
    held = [shards[k] for k in offsets[len(ready) :]]
    _, depth, cells = held[0].shape
    count, width = 2, quads.shape[1] // TILES
    first = [] if begun is None else [pltpu.with_memory_space_constraint(begun, pltpu.VMEM)]
    flops = weigh * 4 * count * width * len(offsets) * depth * 3 * cells
    return whole_call(
        functools.partial(sensitivity_kernel, offsets, len(ready), begun is not None, which, bits),
        "sensitivities",
        jax.ShapeDtypeStruct((cells, count * width), BF16),
        [pltpu.VMEM((3 * cells, len(offsets) * depth), BF16)],
        quads, weight, volume, *([turned] if ready else []), *first, *held,
        flops=flops,
    )


def partial_products(which, bits, quads, turned, offsets):
    rows, total = turned.shape
    count = quads.shape[1] * 2 // TILES
    return whole_call(
        functools.partial(partial_kernel, offsets, which, bits),
        "partial_products",
        pltpu.VMEM((2, rows, count), F32),
        [],
        quads, turned,
        flops=1000,
    )


def same_columns(left, right):
    return lax.dot_general(left, right, (((1,), (1,)), ((), ())), preferred_element_type=F32)


def rows_of(core, cells):
    return pl.ds(pl.multiple_of(core * cells, cells), cells)


def early_kernel(evens, own_send, own_keep, other_send, other_keep, *refs):
    count, (_, chip, core) = len(evens), position()
    recomputed, mine, swap = refs[:count], *refs[count : count + 2]
    mirrors, pair = refs[count + 2 : -1], refs[-1]
    cells = own_send.shape[0]
    here, there = rows_of(core, cells), rows_of(1 - core, cells)
    sides = ((0, own_send, other_send), (1, own_keep, other_keep))
    for at, d in enumerate(evens):
        part = own_send.shape[1] // 2
        for bit in range(2):

            @pl.when(bit_of(chip, low_bit(d)) == bit)
            def _():
                lanes = slice(bit * part, (bit + 1) * part)
                columns = [jnp.concatenate([own[:, lanes], other[:, lanes]], axis=0) for _, own, other in sides]
                blocks = same_columns(recomputed[at][...], jnp.concatenate(columns, axis=1))
                pair[0], pair[1] = jnp.split(blocks, 2, axis=1)

        mine[at] = pair[0]
        swap[at] = pair[1].astype(BF16)
        mirrors[at][here, :] = pair[0].T.astype(BF16)
        mirrors[at][there, :] = pair[1].T.astype(BF16)


def own_kernel(own_send, own_keep, other_send, other_keep, out):
    cells = own_send.shape[0]
    sides = ((own_send[...], other_send[...]), (own_keep[...], other_keep[...]))
    _, _, core = position()
    both = functools.reduce(jnp.add, [same_columns(own, jnp.concatenate([own, other], axis=0)) for own, other in sides])
    out[rows_of(core, cells), :] = both[:, :cells]
    out[rows_of(1 - core, cells), :] = both[:, cells:].T


def late_kernel(odds, own_keep, other_keep, *refs):
    count, (_, _, core) = len(odds), position()
    received, mine, swap, mirrors = refs[:count], refs[count], refs[count + 1], refs[count + 2 :]
    cells = own_keep.shape[0]
    here, there = rows_of(core, cells), rows_of(1 - core, cells)
    rows = jnp.concatenate([r[...] for r in received], axis=0)
    blocks = same_columns(rows, jnp.concatenate([own_keep[...], other_keep[...]], axis=0))
    for at in range(count):
        block, across = jnp.split(blocks[at * cells : (at + 1) * cells], 2, axis=1)
        mine[at] = block
        swap[at] = across.astype(BF16)
        mirrors[at][here, :] = block.astype(BF16).T
        mirrors[at][there, :] = across.astype(BF16).T


def diagonal(cells):
    return lax.broadcasted_iota(I32, (cells, cells), 0) == lax.broadcasted_iota(I32, (cells, cells), 1)


def combine_kernel(evens, odds, own_block, *refs):
    (mine_group, chip, core), every = position(), refs[-1]
    cells = own_block.shape[1]
    here, there = rows_of(core, cells), rows_of(1 - core, cells)
    every[0] = own_block[...]
    at = 0
    for group in (evens, odds):
        mine, swapped, mirrored = refs[at], refs[at + 1], refs[at + 2 : at + 2 + len(group)]
        at += 2 + len(group)
        for i, d in enumerate(group):
            every[d, here, :] = mine[i] + mirrored[i][here, :].astype(F32)
            every[d, there, :] = swapped[i].astype(F32) + mirrored[i][there, :].astype(F32)
    out_own, outs = refs[at], refs[at + 1 : -1]
    first = jnp.bitwise_xor(mine_group, chip)
    out_own[...] = every[first]
    for k, out in enumerate(outs, 1):
        d = jnp.bitwise_xor(first, k)
        out[: 2 * cells, :] = every[d].astype(BF16)
        square = every[d, here, :]
        lost = jnp.where(diagonal(cells), square - square.astype(BF16).astype(F32), 0.0)
        out[2 * cells :, :] = jnp.broadcast_to(jnp.sum(lost, axis=0, keepdims=True), (16, cells)).astype(BF16)


def final_kernel(amount, own, *refs):
    received, out = refs[:-1], refs[-1]
    cells = own.shape[1]
    total = own[...]
    for part in received:
        total = total + part[: 2 * cells, :].astype(F32)
    out[...] = total / amount
    lost = functools.reduce(jnp.add, [part[2 * cells :, :].astype(F32)[:1] for part in received])
    here = rows_of(position()[2], cells)
    out[here, :] += jnp.where(diagonal(cells), lost / amount, 0.0)


def whole_call(kernel, name, shapes, scratch, *arrays, flops=1000):
    vmem = pl.BlockSpec(memory_space=pltpu.VMEM)
    many = isinstance(shapes, list)
    return pl.pallas_call(
        kernel,
        in_specs=[vmem] * len(arrays),
        out_specs=[vmem] * len(shapes) if many else vmem,
        out_shape=shapes,
        scratch_shapes=scratch,
        compiler_params=params(),
        cost_estimate=pl.CostEstimate(flops=flops, bytes_accessed=1, transcendentals=0),
        name=name,
    )(*arrays)


def per_device(grads, quads, volume, weight):
    groups, devices = lax.axis_size("elec"), lax.axis_size("cell")
    chips = devices // 2
    cells, measured = grads.shape[2], quads.shape[0]
    half, far = groups // 2, groups - 1
    odds = [d for d in range(1, chips) if odd(d)]
    evens = [d for d in range(1, chips) if not odd(d)]
    packed, columns = pack(grads, volume, quads.T)
    shape = grads.shape
    gradients = lambda x: x[: 3 * shape[1], :].reshape(shape)
    shards = {0: gradients(packed), far: hop(grads, "elec", groups, far)}
    for j in range(1, half):
        shards[j] = hop(grads, "elec", groups, j)
    for j in range(1, half):
        shards[far ^ j] = hop(shards[far], "elec", groups, j)

    bits = max(1, (chips - 1).bit_length())
    weights = weight.reshape(1, measured)
    volumes = volume.reshape(1, cells)
    relayed = {far ^ j: shards[far ^ j] for j in range(1, half)}
    relayed.update({j: shards[j] for j in range(1, half)})
    direct = {k: shards[k] for k in shards if k not in relayed}
    ready = tuple(sorted(direct))
    turned = turn_shards([direct[k] for k in ready])

    across, volumes_across = {}, {}
    for d in evens:
        near = hop(packed, "cell", devices, 2 * d)
        near, volumes_across[d] = gradients(near), near[3 * shape[1] :, :]
        across[d] = {0: near}
        for k in [far, *range(1, half)]:
            across[d][k] = hop(shards[k], "cell", devices, 2 * d)

    form = functools.partial(sensitivities, bits=bits)
    begun = partial_products("send", bits, columns, turned, ready)
    own_send = form("send", quads=columns, weight=weights, volume=volumes, shards=relayed, begun=begun)
    received = [hop(own_send, "cell", devices, 2 * d) for d in odds]
    other_send = hop(own_send, "cell", devices, 1)
    first = {d: {k: across[d][k] for k in (0, far)} for d in evens}
    columns, own_send, first = lax.optimization_barrier((columns, own_send, first))
    across = {d: {**across[d], **first[d]} for d in evens}
    for d in evens:
        for j in range(1, half):
            across[d][far ^ j] = hop(across[d][far], "elec", groups, j)
    own_keep = form("keep", quads=columns, weight=weights, volume=volumes, shards=relayed, turned=turned, ready=ready)
    other_keep = hop(own_keep, "cell", devices, 1)
    recomputed = []
    for d in evens:
        turned = turn_shards([across[d][k] for k in ready])
        begun = partial_products(d, bits, columns, turned, ready)
        rest = {k: across[d][k] for k in across[d] if k not in ready}
        recomputed.append(
            form(d, quads=columns, weight=weights, volume=volumes_across[d], shards=rest, begun=begun, weigh=WEIGH)
        )

    whole, small = (2 * cells, cells), (cells, cells)
    outputs = lambda group: [
        jax.ShapeDtypeStruct((len(group), *small), F32),
        jax.ShapeDtypeStruct((len(group), *small), BF16),
    ] + [jax.ShapeDtypeStruct(whole, BF16)] * len(group)
    early = whole_call(
        functools.partial(early_kernel, evens),
        "early_blocks",
        outputs(evens),
        [pltpu.VMEM((2, *small), F32)],
        own_send, own_keep, other_send, other_keep, *recomputed,
    )
    late = whole_call(functools.partial(late_kernel, odds), "late_blocks", outputs(odds), [], own_keep, other_keep, *received)

    own_keep, late = lax.optimization_barrier((own_keep, late))
    own_block = whole_call(
        own_kernel, "own_block", jax.ShapeDtypeStruct(whole, F32), [], own_send, own_keep, other_send, other_keep
    )

    def exchange(group, mine, swap, *mirrors):
        moved = [hop(m, "cell", devices, 2 * d) for d, m in zip(group, mirrors)]
        return [mine, hop(swap, "cell", devices, 1)] + moved

    parts = whole_call(
        functools.partial(combine_kernel, evens, odds),
        "combine",
        [jax.ShapeDtypeStruct(whole, F32)] + [jax.ShapeDtypeStruct((2 * cells + 16, cells), BF16)] * (groups - 1),
        [pltpu.VMEM((chips, *whole), F32)],
        own_block, *exchange(evens, *early), *exchange(odds, *late),
    )
    arrived = [hop(parts[k], "elec", groups, k) for k in sorted(range(1, groups), key=lambda k: (k < half, -k))]
    return whole_call(
        functools.partial(final_kernel, float(measured * groups)),
        "finish",
        jax.ShapeDtypeStruct(whole, F32),
        [],
        parts[0], *arrived,
    )


def solution(mesh):
    placed = (P(None, "elec", "cell"), P("elec", None), P("cell"), P("elec"))
    return jax.shard_map(
        per_device, mesh=mesh, in_specs=placed, out_specs=P("elec", "cell"), check_vma=False
    )
```
